128 devices in a mesh: seq: 32 (over z_hi, y, x), tp: 4 (over z_lo, core).
Axes of the slice: x: 4, y: 4, z: 4 (z_hi: 2, z_lo: 2; z = z_hi * 2 + z_lo), core: 2. Of those that a mesh axis runs over, the one named last changes fastest.
Arguments:
- tokens: bfloat16 [12288, 5376], P('seq', 'tp'), may hold values from -6 to 6
- positions: int32 [12288], P('seq'), may hold values from 0 to 2047, as said below
- w_query: bfloat16 [5376, 3072], P(None, 'tp'), may hold values from -0.078125 to 0.078125
- w_key: bfloat16 [5376, 1536], P(None, 'tp'), may hold values from -0.078125 to 0.078125
- w_value: bfloat16 [5376, 1536], P(None, 'tp'), may hold values from -0.078125 to 0.078125
- w_out: bfloat16 [3072, 5376], P('tp'), may hold values from -0.25 to 0.25
- gain_input: float32 [5376], replicated, may hold values from 0.5 to 1.5
- gain_query: float32 [128], replicated, may hold values from 0.5 to 1.5
- gain_key: float32 [128], replicated, may hold values from 0.5 to 1.5
- gain_post: float32 [5376], replicated, may hold values from 0.5 to 1.5
- gain_pre: float32 [5376], replicated, may hold values from 0.5 to 1.5
Outputs:
- hidden: bfloat16 [12288, 5376], P('seq', 'tp')
- ffn_input: bfloat16 [12288, 5376], P('seq', 'tp')
The draws below stay inside these ranges and needn't reach their ends.
Inputs may be any that keep to these rules, and one draw needn't show every extreme that they name: positions[0] is 0, and every later entry is either 0 (a document starts there) or the entry before it plus 1; no document is longer than 2048 tokens.
All inputs are finite; a program needn't handle non-finite values.
Results may differ from the reference program's by a relative error of at most 0.0096.
Values may be sent and summed in bfloat16 or wider, within the bound.
A program may use at most 128 MiB of HBM per device.

```python
import jax
import jax.numpy as jnp
from jax import lax

D = 5376
HEADS = 24
KV_HEADS = 12
HEAD_DIM = 128
WINDOW = 1024
TOK_DEV = 384
TOKENS = 12288
N_SEQ = 32


def draw_positions(key, part):
    index = jnp.arange(TOKENS, dtype=jnp.int32)
    longest = min(2 * WINDOW, TOKENS // 2)
    spread = min(3 * WINDOW // 2, max(TOKENS // 4, 2))
    offset_rows = index - 3
    marks = jax.random.randint(jax.random.fold_in(key, 11), (TOKENS,), 0, spread)
    chosen = jax.random.randint(jax.random.fold_in(key, 12), (), 0, (TOKENS - 3) // longest)
    forced = (offset_rows % longest == 0) | (index == 0)
    inside = (offset_rows // longest == chosen) & (offset_rows % longest != 0)
    middle_zone = (index > TOKENS // 2 - WINDOW - TOK_DEV) & (index < TOKENS // 2 + TOK_DEV)
    starts = (marks == 0) & jnp.logical_not(inside) & jnp.logical_not(middle_zone) | forced
    last_start = lax.cummax(jnp.where(starts, index, 0), axis=0)
    return (index - last_start).astype(jnp.int32)


def draw_w_out(key, part):
    row_count = HEADS * HEAD_DIM
    col_frac = jnp.arange(D, dtype=jnp.float32) / D
    rough = jax.random.uniform(jax.random.fold_in(key, 21), (D,), jnp.float32, 0.6, 1.5)
    base = jax.random.truncated_normal(jax.random.fold_in(key, 23), -4.0, 4.0, (row_count, D), jnp.float32)
    trend = 3.0 ** col_frac
    scales = trend * rough
    scales = scales / jnp.sqrt(jnp.mean(scales * scales))
    drawn = base * scales[None, :] / jnp.sqrt(jnp.float32(row_count))
    return jnp.clip(drawn, -0.25, 0.25).astype(jnp.bfloat16)


def levels(rng, dims, split, smallest, top_value):
    def one(position, parts):
        heights = jax.random.uniform(jax.random.fold_in(jax.random.fold_in(rng, 6), position), (parts,), jnp.float32, smallest / len(split), top_value / len(split))
        return jnp.repeat(jnp.exp(heights), dims[position] // parts).reshape((-1,) + (1,) * (len(dims) - position - 1))

    factor_of = one(*split[0])
    for cut in split[1:]:
        factor_of = factor_of * one(*cut)
    return factor_of


def bell_draw(rng, shape, width, most, shards=(), kind=jnp.bfloat16):
    array = width * jax.random.normal(rng, shape, jnp.float32)
    if shards:
        array = array * levels(rng, shape, shards, -0.22, 0.18)
    return jnp.clip(array, -most, most).astype(kind)


def setup_inputs(seed: int = 0) -> dict:
    splits = jax.random.split(jax.random.key(seed), 12)
    tokens = bell_draw(splits[0], (TOKENS, D), 1.0, 6.0, ((0, 32), (1, 4)))
    positions = draw_positions(jax.random.fold_in(splits[11], 71), 0)
    w_query = bell_draw(splits[2], (D, HEADS * HEAD_DIM), D ** -0.5, 0.078125, ((1, 4),))
    w_key = bell_draw(splits[3], (D, KV_HEADS * HEAD_DIM), D ** -0.5, 0.078125, ((1, 4),))
    w_value = bell_draw(splits[4], (D, KV_HEADS * HEAD_DIM), D ** -0.5, 0.078125, ((1, 4),))
    w_out = draw_w_out(jax.random.fold_in(splits[11], 71), 0)
    gain_input = jnp.clip(1.0 + 0.1 * jax.random.normal(splits[6], (D,), jnp.float32), 0.5, 1.5)
    gain_query = jnp.clip(1.0 + 0.1 * jax.random.normal(splits[7], (HEAD_DIM,), jnp.float32), 0.5, 1.5)
    gain_key = jnp.clip(1.0 + 0.1 * jax.random.normal(splits[8], (HEAD_DIM,), jnp.float32), 0.5, 1.5)
    gain_post = jnp.clip(1.0 + 0.1 * jax.random.normal(splits[9], (D,), jnp.float32), 0.5, 1.5)
    gain_pre = jnp.clip(1.0 + 0.1 * jax.random.normal(splits[10], (D,), jnp.float32), 0.5, 1.5)
    return dict(tokens=tokens, positions=positions, w_query=w_query, w_key=w_key, w_value=w_value, w_out=w_out, gain_input=gain_input, gain_query=gain_query, gain_key=gain_key, gain_post=gain_post, gain_pre=gain_pre)


norm_eps = 1e-06
query_scale = 168.0 ** (-0.5)
rope_base = 10000.0

def rms_scale(field, weight_gain):
    square_mean = lax.optimization_barrier(jnp.mean(field * field, axis=-1, keepdims=True))
    return field * lax.rsqrt(square_mean + norm_eps) * weight_gain

def rotate(field, positions):
    half_dim = field.shape[-1] // 2
    inverse_freq = jnp.exp(-jnp.log(rope_base) * jnp.arange(half_dim, dtype=jnp.float32) / half_dim)
    angles = positions.astype(jnp.float32)[:, None] * inverse_freq[None, :]
    cosine = jnp.cos(angles)[:, None, :]
    sine = jnp.sin(angles)[:, None, :]
    first_half = field[..., :half_dim]
    second_half = field[..., half_dim:]
    return jnp.concatenate([first_half * cosine - second_half * sine, second_half * cosine + first_half * sine], axis=-1)

def head_project(normed, weight, weight_gain, positions):
    projected = jnp.dot(normed, weight, preferred_element_type=jnp.float32)
    projected = projected.reshape(normed.shape[0], -1, HEAD_DIM)
    return rotate(rms_scale(projected, weight_gain), positions).astype(jnp.bfloat16)

def reference(tokens, positions, w_query, w_key, w_value, w_out, gain_input, gain_query, gain_key, gain_post, gain_pre):
    normed = rms_scale(tokens.astype(jnp.float32), gain_input).astype(jnp.bfloat16)
    query_rows = head_project(normed, w_query, gain_query, positions)
    key_rows = head_project(normed, w_key, gain_key, positions)
    value_rows = jnp.dot(normed, w_value, preferred_element_type=jnp.float32).astype(jnp.bfloat16)
    value_rows = value_rows.reshape(TOKENS, KV_HEADS, HEAD_DIM)
    padding = jnp.zeros((WINDOW, KV_HEADS, HEAD_DIM), jnp.bfloat16)
    key_padded = jnp.concatenate([padding, key_rows], axis=0)
    value_padded = jnp.concatenate([padding, value_rows], axis=0)
    groups = HEADS // KV_HEADS

    def one_block(block):
        start = (block * TOK_DEV).astype(jnp.int32)
        query_block = lax.dynamic_slice_in_dim(query_rows, start, TOK_DEV, 0).reshape(TOK_DEV, KV_HEADS, groups, HEAD_DIM)
        key_block = lax.dynamic_slice_in_dim(key_padded, start, TOK_DEV + WINDOW, 0)
        value_block = lax.dynamic_slice_in_dim(value_padded, start, TOK_DEV + WINDOW, 0)
        position_block = lax.dynamic_slice_in_dim(positions, start, TOK_DEV, 0)
        query_index = start + jnp.arange(TOK_DEV, dtype=jnp.int32)
        key_index = start - WINDOW + jnp.arange(TOK_DEV + WINDOW, dtype=jnp.int32)
        doc_start = query_index - position_block
        visible = (key_index[None, :] >= doc_start[:, None]) & (key_index[None, :] > query_index[:, None] - WINDOW) & (key_index[None, :] <= query_index[:, None])
        scores = jnp.einsum('tkgd,skd->kgts', query_block.astype(jnp.float32), key_block.astype(jnp.float32)) * query_scale
        weights = jnp.where(visible[None, None], jnp.exp(scores), 0.0)
        totals = lax.optimization_barrier(jnp.sum(weights, axis=-1))
        weights_low = weights.astype(jnp.bfloat16)
        numer = jnp.einsum('kgts,skd->tkgd', weights_low.astype(jnp.float32), value_block.astype(jnp.float32))
        attended = numer / jnp.transpose(totals, (2, 0, 1))[..., None]
        return attended.astype(jnp.bfloat16).reshape(TOK_DEV, HEADS * HEAD_DIM)
    attended = lax.map(one_block, jnp.arange(N_SEQ, dtype=jnp.int32)).reshape(TOKENS, HEADS * HEAD_DIM)
    summed = jnp.dot(attended, w_out, preferred_element_type=jnp.float32)
    hidden = (tokens.astype(jnp.float32) + rms_scale(summed, gain_post)).astype(jnp.bfloat16)
    ffn_input = rms_scale(hidden.astype(jnp.float32), gain_pre).astype(jnp.bfloat16)
    return (hidden, ffn_input)
```

```python
import functools
import math

import jax
import jax.numpy as jnp
from jax import lax
from jax.experimental import pallas as pl
from jax.experimental.pallas import tpu as pltpu
from jax.sharding import Mesh
from jax.sharding import PartitionSpec as P

F32 = jnp.float32
BF16 = jnp.bfloat16
MESH = pl.DeviceIdType.MESH

EPS = 1e-6
WIDTH = 5376
OWN = 1344
HALF = 672
PAD = 1408
ROWS = 384
CH = 128
NC = 3
KV = 768
N_SEQ = 32
SCORE = 168.0**-0.5 * math.log2(math.e)


def kernel(
    xt, pos, wq, wk, wv, wo, gi, gq, gk, gpost, gpre,
    hid, ffn,
    xg, wqv, wkv, wvv, wov, acc, ss, gtab, rope_c, rope_s, bias,
    qs, kvb, o_acc, l_acc, att, rs_send, rs_recv, own, tok, st_send, st_recv,
    s_own, s_sib, r_sib, s_z, r_z, s_f, r_f, s_w, s_wo, s_wos, r_wos,
    s_kv, r_kv, s_at, r_at, s_rs, r_rs, s_st, r_st,
):
    seq = lax.axis_index("seq")
    zl = lax.axis_index("tp_0")
    core = lax.axis_index("tp_1")

    def peer(k):
        return (seq, lax.rem(zl + k // 2, 2), lax.rem(core + k % 2, 2))

    def tp_of(k):
        return lax.rem(zl + k // 2, 2) * 2 + lax.rem(core + k % 2, 2)

    def col_start(k):
        t = tp_of(k)
        return pl.multiple_of(OWN * t - 64 * lax.rem(t, 2), 128)

    def later(k):
        return (lax.rem(seq + k, N_SEQ), zl, core)

    barrier = pltpu.get_barrier_semaphore()
    for k in (1, 2, 3):
        pl.semaphore_signal(barrier, inc=1, device_id=peer(k), device_id_type=MESH)
        pl.semaphore_signal(barrier, inc=1, device_id=later(k), device_id_type=MESH)
        pl.semaphore_signal(barrier, inc=1, device_id=later(N_SEQ - k), device_id_type=MESH)
    pl.semaphore_wait(barrier, 9)

    def remote(src, dst, ss_, rs_, dev):
        return pltpu.make_async_remote_copy(
            src_ref=src, dst_ref=dst, send_sem=ss_, recv_sem=rs_, device_id=dev, device_id_type=MESH
        )

    def piece(ref, c, h):
        return ref.at[pl.ds(h * HALF, HALF), pl.ds(c * CH, CH)]

    def z_copy(c, h):
        return remote(piece(xt, c, h), piece(xg.at[2], c, h), s_z.at[c, h], r_z.at[c, h], peer(2))

    def f_copy(c, h):
        return remote(piece(xg.at[2], c, h), piece(xg.at[3], c, h), s_f.at[c, h], r_f.at[c, h], peer(1))

    sib_copy = remote(xt, xg.at[1], s_sib, r_sib, peer(1))
    own_copy = pltpu.make_async_copy(xt, xg.at[0], s_own)

    def w_copies(k):
        first = pl.multiple_of(tp_of(k) * OWN, 16)
        return [
            pltpu.make_async_copy(a.at[pl.ds(first, OWN)], b.at[k], s_w.at[i, k])
            for i, (a, b) in enumerate(((wq, wqv), (wk, wkv), (wv, wvv)))
        ]

    wo_copies = [
        pltpu.make_async_copy(wo.at[:, pl.ds(col_start(k), PAD)], wov.at[i, pl.ds(0, KV)], s_wo.at[i])
        for i, k in enumerate((2, 0))
    ]
    wo_remote = [
        remote(wo.at[:, pl.ds(col_start(k), PAD)], wov.at[i, pl.ds(KV, KV)], s_wos.at[i], r_wos.at[i], peer(1))
        for i, k in enumerate((3, 1))
    ]

    def kv_copy(k, c):
        return remote(
            kvb.at[c, pl.ds(3 * CH, CH)],
            kvb.at[c, pl.ds((3 - k) * CH, CH)],
            s_kv.at[k - 1, c],
            r_kv.at[k - 1, c],
            later(k),
        )

    def att_copy(c):
        return remote(
            att.at[pl.ds(c * CH, CH), pl.ds(0, KV)],
            att.at[pl.ds(c * CH, CH), pl.ds(KV, KV)],
            s_at.at[c],
            r_at.at[c],
            peer(1),
        )

    def rs_copy(c):
        return remote(rs_send.at[c], rs_recv.at[c], s_rs.at[c], r_rs.at[c], peer(2))

    def st_copy(c, k):
        return remote(st_send.at[c], st_recv.at[c, k - 1], s_st.at[c, k - 1], r_st.at[c, k - 1], peer(k))

    for c in range(NC):
        for h in range(2):
            z_copy(c, h).start()
    own_copy.start()
    sib_copy.start()
    for k in range(4):
        for cp in w_copies(k):
            cp.start()
    for cp in wo_copies + wo_remote:
        cp.start()

    acc[...] = jnp.zeros_like(acc)
    ss[...] = jnp.zeros_like(ss)
    o_acc[...] = jnp.zeros_like(o_acc)
    l_acc[...] = jnp.zeros_like(l_acc)
    for k in (1, 2, 3):
        @pl.when(seq < k)
        def _():
            for c in range(NC):
                kvb[c, pl.ds((3 - k) * CH, CH), :] = jnp.zeros((CH, KV), BF16)
    kvb[0, pl.ds(0, CH), :] = jnp.zeros((CH, KV), BF16)

    for i in range(8):
        gtab[i] = jnp.broadcast_to(gi[:, pl.ds(i * HALF, HALF)], (8, HALF))

    lane = lax.broadcasted_iota(jnp.int32, (CH, CH), 1)
    sub = lax.broadcasted_iota(jnp.int32, (CH, CH), 0)
    half_lane = jnp.where(lane >= 64, lane - 64, lane).astype(F32)
    inverse_freq = jnp.exp(half_lane * (-math.log(10000.0) / 64))
    for c in range(NC):
        p_row = pos[:, pl.ds(c * CH, CH)].astype(F32)
        p_mat = jnp.broadcast_to(p_row, (CH, CH)).T
        angle = p_mat * inverse_freq
        sine = jnp.sin(angle)
        rope_c[c] = jnp.cos(angle)
        rope_s[c] = jnp.where(lane < 64, -sine, sine)
        i_rel = sub + c * CH
        low = i_rel - jnp.minimum(p_mat.astype(jnp.int32), 1023)
        for cc in range(NC):
            first = 3 if cc > c else 2
            for n in range(3):
                j_rel = CH * cc + ROWS * (n - first) + lane
                bias[c, cc, :, pl.ds(n * CH, CH)] = jnp.where((j_rel >= low) & (j_rel <= i_rel), 0.0, -1e30)

    own_copy.wait()
    for c in range(NC):
        x = xg[0, :, pl.ds(c * CH, CH)].astype(F32).T
        x = jnp.concatenate([x, jnp.zeros((CH, PAD - OWN), F32)], axis=1)
        tok[pl.ds(c * CH, CH), :] = jnp.where(core == 1, pltpu.roll(x, 64, 1), x)

    def step(k, c, h):
        cols = pl.ds(pl.multiple_of(c * CH, CH), CH)
        feats = pl.ds(pl.multiple_of(h * HALF, 16), HALF)
        x = xg[k, feats, cols].astype(F32)
        ss[c] += jnp.broadcast_to(jnp.sum(x * x, axis=0, keepdims=True), (8, CH))
        gain = gtab[tp_of(k) * 2 + h, pl.ds(0, 1), :]
        x = (x.T * gain).astype(BF16)
        acc[cols, pl.ds(0, 768)] += jnp.dot(x, wqv[k, feats, :], preferred_element_type=F32)
        acc[cols, pl.ds(768, 384)] += jnp.dot(x, wkv[k, feats, :], preferred_element_type=F32)
        acc[cols, pl.ds(1152, 384)] += jnp.dot(x, wvv[k, feats, :], preferred_element_type=F32)

    def local_steps(k):
        for cp in w_copies(k):
            cp.wait()

        @pl.loop(0, NC * 2)
        def _(i):
            step(k, i // 2, lax.rem(i, 2))

    local_steps(0)
    sib_copy.wait_recv()
    local_steps(1)
    for k in (2, 3):
        for cp in w_copies(k):
            cp.wait()

    def head(u, gain, c):
        mean = jnp.mean(u * u, axis=-1, keepdims=True)
        u = u * lax.rsqrt(mean + EPS) * gain
        return (u * rope_c[c] + pltpu.roll(u, 64, 1) * rope_s[c]).astype(BF16)

    def finish(c):
        rows = pl.ds(c * CH, CH)
        mean = ss[c, pl.ds(0, 1), :] / WIDTH
        scale = jnp.broadcast_to(lax.rsqrt(mean + EPS), (CH, CH)).T
        for h in range(3):
            u = acc[rows, pl.ds(768 + h * 128, 128)] * scale
            kvb[c, pl.ds(3 * CH, CH), pl.ds(h * 128, 128)] = head(u, gk[...], c)
            v = acc[rows, pl.ds(1152 + h * 128, 128)] * scale
            kvb[c, pl.ds(3 * CH, CH), pl.ds(384 + h * 128, 128)] = v.astype(BF16)
        for k in (1, 2, 3):
            if k == 3 and c == 0:
                continue

            @pl.when(seq + k < N_SEQ)
            def _():
                kv_copy(k, c).start()
        for h in range(3):
            for g in range(2):
                u = acc[rows, pl.ds((2 * h + g) * 128, 128)] * scale
                qs[c, h, pl.ds(g * CH, CH), :] = head(u, gq[...], c)

    for c in range(NC):
        @pl.loop(0, 2)
        def _(h):
            z_copy(c, h).wait_recv()
            f_copy(c, h).start()
            step(2, c, h)
            f_copy(c, h).wait_recv()
            step(3, c, h)

        finish(c)

    def unit(c, cc):
        start = 0 if cc > c else CH
        b = bias[c, cc]
        b = jnp.concatenate([b, b], axis=0)
        for h in range(3):
            keys = kvb[cc, pl.ds(start, 3 * CH), pl.ds(h * 128, 128)]
            vals = kvb[cc, pl.ds(start, 3 * CH), pl.ds(384 + h * 128, 128)]
            s = lax.dot_general(qs[c, h], keys, (((1,), (1,)), ((), ())), preferred_element_type=F32)
            w = jnp.exp2(s * SCORE + b)
            l_acc[c, h] += w[:, 0:128] + w[:, 128:256] + w[:, 256:384]
            o_acc[c, h] += jnp.dot(w.astype(BF16), vals, preferred_element_type=F32)

    def kv_arrived(cc):
        for k in (1, 2, 3):
            if k == 3 and cc == 0:
                continue

            @pl.when(seq >= k)
            def _():
                kv_copy(k, cc).wait_recv()

    for cc in range(2):
        kv_arrived(cc)
        for c in range(NC):
            unit(c, cc)
    kv_arrived(2)
    for cp in wo_copies:
        cp.wait()
    for cp in wo_remote:
        cp.wait()

    def project(c, i):
        return jnp.dot(att[pl.ds(c * CH, CH), :], wov[i], preferred_element_type=F32)

    for c in range(NC):
        unit(c, 2)
        for h in range(3):
            total = jnp.sum(l_acc[c, h], axis=-1, keepdims=True)
            o = (o_acc[c, h] / total).astype(BF16)
            att[pl.ds(c * CH, CH), pl.ds(2 * h * 128, 128)] = o[:CH]
            att[pl.ds(c * CH, CH), pl.ds((2 * h + 1) * 128, 128)] = o[CH:]
        att_copy(c).start()
        if c > 0:
            att_copy(c - 1).wait_recv()
            rs_send[c - 1] = project(c - 1, 0).astype(BF16)
            rs_copy(c - 1).start()
    att_copy(2).wait_recv()
    rs_send[2] = project(2, 0).astype(BF16)
    rs_copy(2).start()

    for c in range(NC):
        own[pl.ds(c * CH, CH), :] = project(c, 1)

    gain_post = gpost[:, pl.ds(col_start(0), PAD)]
    gain_pre = gpre[:, pl.ds(col_start(0), PAD)]
    col = lax.broadcasted_iota(jnp.int32, (1, PAD), 1) - 64 * core
    inside = ((col >= 0) & (col < OWN)).astype(F32)

    def stats(c):
        rows = pl.ds(c * CH, CH)
        rs_copy(c).wait_recv()
        s = (own[rows, :] + rs_recv[c].astype(F32)) * inside
        own[rows, :] = s
        t = tok[rows, :]
        sg = s * gain_post
        both = [jnp.sum(v, axis=-1, keepdims=True) for v in (s * s, t * t, t * sg, sg * sg)]
        table = jnp.where(lane == 0, both[0], jnp.where(lane == 1, both[1], jnp.where(lane == 2, both[2], both[3])))
        st_send[c] = table.T[0:8, :]
        for k in (1, 2, 3):
            st_copy(c, k).start()

    def final(c):
        rows = pl.ds(c * CH, CH)
        for k in (1, 2, 3):
            st_copy(c, k).wait_recv()
        rows4 = st_send[c] + st_recv[c, 0] + st_recv[c, 1] + st_recv[c, 2]
        post = lax.rsqrt(rows4[0:1] / WIDTH + EPS)
        square = rows4[1:2] + 2.0 * post * rows4[2:3] + post * post * rows4[3:4]
        pre = lax.rsqrt(jnp.maximum(square, 0.0) / WIDTH + EPS)
        post = jnp.broadcast_to(post, (CH, CH)).T[:, 0:1]
        pre = jnp.broadcast_to(pre, (CH, CH)).T[:, 0:1]
        hidden = (tok[rows, :] + own[rows, :] * post * gain_post).astype(BF16).astype(F32)
        out = hidden * pre * gain_pre

        def place(v):
            return jnp.where(core == 1, pltpu.roll(v, PAD - 64, 1), v)[:, :OWN].astype(BF16)

        hid[rows, :] = place(hidden)
        ffn[rows, :] = place(out)

    for c in range(NC):
        stats(c)
        final(c)

    sib_copy.wait_send()
    for c in range(NC):
        for h in range(2):
            z_copy(c, h).wait_send()
            f_copy(c, h).wait_send()
        for k in (1, 2, 3):
            if not (k == 3 and c == 0):
                @pl.when(seq + k < N_SEQ)
                def _():
                    kv_copy(k, c).wait_send()
            st_copy(c, k).wait_send()
        att_copy(c).wait_send()
        rs_copy(c).wait_send()


def local(tokens, positions, w_query, w_key, w_value, w_out, gain_input, gain_query, gain_key, gain_post, gain_pre):
    hbm = pl.BlockSpec(memory_space=pltpu.MemorySpace.HBM)
    vmem = pl.BlockSpec(memory_space=pltpu.VMEM)
    dma = pltpu.SemaphoreType.DMA
    out = jax.ShapeDtypeStruct((ROWS, OWN), BF16)
    return pl.pallas_call(
        kernel,
        out_shape=(out, out),
        in_specs=[hbm, vmem, hbm, hbm, hbm, hbm, vmem, vmem, vmem, vmem, vmem],
        out_specs=(vmem, vmem),
        scratch_shapes=[
            pltpu.VMEM((4, OWN, ROWS), BF16),
            pltpu.VMEM((4, OWN, 768), BF16),
            pltpu.VMEM((4, OWN, 384), BF16),
            pltpu.VMEM((4, OWN, 384), BF16),
            pltpu.VMEM((2, 2 * KV, PAD), BF16),
            pltpu.VMEM((ROWS, 1536), F32),
            pltpu.VMEM((NC, 8, CH), F32),
            pltpu.VMEM((8, 8, HALF), F32),
            pltpu.VMEM((NC, CH, CH), F32),
            pltpu.VMEM((NC, CH, CH), F32),
            pltpu.VMEM((NC, NC, CH, 3 * CH), F32),
            pltpu.VMEM((NC, 3, 2 * CH, 128), BF16),
            pltpu.VMEM((NC, 4 * CH, KV), BF16),
            pltpu.VMEM((NC, 3, 2 * CH, 128), F32),
            pltpu.VMEM((NC, 3, 2 * CH, 128), F32),
            pltpu.VMEM((ROWS, 2 * KV), BF16),
            pltpu.VMEM((NC, CH, PAD), BF16),
            pltpu.VMEM((NC, CH, PAD), BF16),
            pltpu.VMEM((ROWS, PAD), F32),
            pltpu.VMEM((ROWS, PAD), F32),
            pltpu.VMEM((NC, 8, CH), F32),
            pltpu.VMEM((NC, 3, 8, CH), F32),
            dma, dma, dma,
            dma((NC, 2)), dma((NC, 2)), dma((NC, 2)), dma((NC, 2)),
            dma((3, 4)), dma((2,)), dma((2,)), dma((2,)),
            dma((3, NC)), dma((3, NC)),
            dma((NC,)), dma((NC,)), dma((NC,)), dma((NC,)),
            dma((NC, 3)), dma((NC, 3)),
        ],
        compiler_params=pltpu.CompilerParams(
            collective_id=0, has_side_effects=True, vmem_limit_bytes=60 * 1024 * 1024
        ),
        cost_estimate=pl.CostEstimate(flops=12_000_000_000, bytes_accessed=28_000_000, transcendentals=3_000_000),
    )(
        tokens.T,
        positions.reshape(1, ROWS),
        w_query,
        w_key,
        w_value,
        w_out,
        gain_input.reshape(1, WIDTH),
        gain_query.reshape(1, 128),
        gain_key.reshape(1, 128),
        gain_post.reshape(1, WIDTH),
        gain_pre.reshape(1, WIDTH),
    )


def solution(mesh):
    torus = Mesh(mesh.devices.reshape(N_SEQ, 2, 2), ("seq", "tp_0", "tp_1"))
    tp = ("tp_0", "tp_1")
    return jax.shard_map(
        local,
        mesh=torus,
        in_specs=(
            P("seq", tp), P("seq"), P(None, tp), P(None, tp), P(None, tp), P(tp, None),
            P(), P(), P(), P(), P(),
        ),
        out_specs=(P("seq", tp), P("seq", tp)),
        check_vma=False,
    )
```

```python
import functools
import math

import jax
import jax.numpy as jnp
from jax import lax
from jax.experimental import pallas as pl
from jax.experimental.pallas import tpu as pltpu
from jax.sharding import Mesh
from jax.sharding import PartitionSpec as P

F32 = jnp.float32
BF16 = jnp.bfloat16
MESH = pl.DeviceIdType.MESH

EPS = 1e-6
WIDTH = 5376
OWN = 1344
HALF = 672
PAD = 1408
ROWS = 384
CH = 128
NC = 3
KV = 768
N_SEQ = 32
SCORE = 168.0**-0.5 * math.log2(math.e)


def kernel(
    xt, pos, wq, wk, wv, wo, gi, gq, gk, gpost, gpre,
    hid, ffn,
    xg, wqv, wkv, wvv, wov, acc, ss, gtab, rope_c, rope_s, bias,
    qs, kvb, o_acc, l_acc, att, rs_send, rs_recv, own, tok, st_send, st_recv, stage,
    s_own, s_sib, r_sib, s_z, r_z, s_f, r_f, s_w, s_wo, s_wos, r_wos,
    s_kv, r_kv, s_stage, r_stage, s_pass, r_pass, s_at, r_at, s_rs, r_rs, s_st, r_st,
):
    seq = lax.axis_index("seq")
    zl = lax.axis_index("tp_0")
    core = lax.axis_index("tp_1")

    def peer(k):
        return (seq, lax.rem(zl + k // 2, 2), lax.rem(core + k % 2, 2))

    def tp_of(k):
        return lax.rem(zl + k // 2, 2) * 2 + lax.rem(core + k % 2, 2)

    def col_start(k):
        t = tp_of(k)
        return pl.multiple_of(OWN * t - 64 * lax.rem(t, 2), 128)

    def later(k, dz=0):
        return (lax.rem(seq + k, N_SEQ), lax.rem(zl + dz, 2), core)

    barrier = pltpu.get_barrier_semaphore()
    for k in (1, 2, 3):
        pl.semaphore_signal(barrier, inc=1, device_id=peer(k), device_id_type=MESH)
    for k in (1, 3, N_SEQ - 1, N_SEQ - 3):
        for dz in (0, 1):
            pl.semaphore_signal(barrier, inc=1, device_id=later(k, dz), device_id_type=MESH)
    pl.semaphore_wait(barrier, 11)

    def remote(src, dst, ss_, rs_, dev):
        return pltpu.make_async_remote_copy(
            src_ref=src, dst_ref=dst, send_sem=ss_, recv_sem=rs_, device_id=dev, device_id_type=MESH
        )

    def piece(ref, c, h):
        return ref.at[pl.ds(h * HALF, HALF), pl.ds(c * CH, CH)]

    def z_copy(c, h):
        return remote(piece(xt, c, h), piece(xg.at[2], c, h), s_z.at[c, h], r_z.at[c, h], peer(2))

    def f_copy(c, h):
        return remote(piece(xg.at[2], c, h), piece(xg.at[3], c, h), s_f.at[c, h], r_f.at[c, h], peer(1))

    sib_copy = remote(xt, xg.at[1], s_sib, r_sib, peer(1))
    own_copy = pltpu.make_async_copy(xt, xg.at[0], s_own)

    def w_copies(k):
        first = pl.multiple_of(tp_of(k) * OWN, 16)
        return [
            pltpu.make_async_copy(a.at[pl.ds(first, OWN)], b.at[k], s_w.at[i, k])
            for i, (a, b) in enumerate(((wq, wqv), (wk, wkv), (wv, wvv)))
        ]

    wo_copies = [
        pltpu.make_async_copy(wo.at[:, pl.ds(col_start(k), PAD)], wov.at[i, pl.ds(0, KV)], s_wo.at[i])
        for i, k in enumerate((2, 0))
    ]
    wo_remote = [
        remote(wo.at[:, pl.ds(col_start(k), PAD)], wov.at[i, pl.ds(KV, KV)], s_wos.at[i], r_wos.at[i], peer(1))
        for i, k in enumerate((3, 1))
    ]

    def kv_copy(back, ahead, c):
        far = (back + ahead) % N_SEQ
        return remote(
            kvb.at[c, pl.ds((3 - back) * CH, CH)],
            kvb.at[c, pl.ds((3 - far) * CH, CH)],
            s_kv.at[3 if back == 3 else far - 1, c],
            r_kv.at[far - 1, c],
            later(ahead),
        )

    seq16 = lax.rem(seq, 16)
    crossing = (seq16 >= 13) & (seq < 16)

    def key_copy(ahead, c):
        return remote(
            kvb.at[c, pl.ds(3 * CH, CH), pl.ds(0, 384)],
            kvb.at[c, pl.ds((3 - ahead) * CH, CH), pl.ds(0, 384)],
            s_kv.at[ahead - 1, c],
            r_kv.at[ahead - 1, c],
            later(ahead),
        )

    def value_copy(ahead, c):
        return remote(
            kvb.at[c, pl.ds(3 * CH, CH), pl.ds(384, 384)],
            stage.at[ahead // 2, c],
            s_stage.at[ahead // 2, c],
            r_stage.at[ahead // 2, c],
            later(ahead, 1),
        )

    def value_pass(ahead, c):
        return remote(
            stage.at[ahead // 2, c],
            kvb.at[c, pl.ds((3 - ahead) * CH, CH), pl.ds(384, 384)],
            s_pass.at[ahead // 2, c],
            r_pass.at[ahead // 2, c],
            peer(2),
        )

    def sends(ahead, c):
        if ahead == 3 and c == 0:
            return seq == 14
        return seq < N_SEQ - ahead

    def crosses(ahead, c):
        if ahead == 1:
            return seq == 15
        return (seq == 14) if c == 0 else crossing

    def crossed(ahead, c):
        if ahead == 1:
            return seq == 16
        return (seq == 17) if c == 0 else (seq >= 16) & (seq < 19)

    def relays_on(c):
        on = (seq >= 1) & (seq < N_SEQ - 1)
        return on & (seq != 15) if c == 0 else on & (seq16 == 14)

    def relays_back(c):
        return (seq == 17) if c == 0 else (seq >= 3) & (seq16 != 0)

    def send_kv(ahead, c):
        @pl.when(sends(ahead, c) & jnp.logical_not(crosses(ahead, c)))
        def _():
            kv_copy(0, ahead, c).start()

    def send_values(ahead, c):
        @pl.when(crosses(ahead, c))
        def _():
            value_copy(ahead, c).start()

    def send_keys(ahead, c):
        @pl.when(crosses(ahead, c))
        def _():
            key_copy(ahead, c).start()

    def pass_values(ahead, c):
        @pl.when(crossed(ahead, c))
        def _():
            value_copy(ahead, c).wait_recv()
            value_pass(ahead, c).start()

    def got_kv(ahead, c, other):
        @pl.when(other & crossed(ahead, c))
        def _():
            key_copy(ahead, c).wait_recv()
            value_pass(ahead, c).wait_recv()

        first = (seq >= 1) if ahead == 1 else (seq >= 3) if c > 0 else (seq < 0)

        @pl.when(other & first & jnp.logical_not(crossed(ahead, c)))
        def _():
            kv_copy(0, ahead, c).wait_recv()

    def relay_on(c, some=True):
        got_kv(1, c, relays_on(c) & some)

        @pl.when(relays_on(c) & some)
        def _():
            kv_copy(1, 1, c).start()

    def relay_back(c):
        got_kv(3, c, relays_back(c))

        @pl.when(relays_back(c))
        def _():
            kv_copy(3, N_SEQ - 1, c).start()

    def kv_arrived(c):
        got_kv(1, c, jnp.logical_not(relays_on(c)))

        @pl.when(seq >= 2)
        def _():
            kv_copy(1, 1, c).wait_recv()

        got_kv(3, c, jnp.logical_not(relays_back(c)))

    def kv_left(c):
        for ahead in (1, 3):
            @pl.when(sends(ahead, c) & jnp.logical_not(crosses(ahead, c)))
            def _():
                kv_copy(0, ahead, c).wait_send()

            @pl.when(crosses(ahead, c))
            def _():
                value_copy(ahead, c).wait_send()
                key_copy(ahead, c).wait_send()

            @pl.when(crossed(ahead, c))
            def _():
                value_pass(ahead, c).wait_send()

        @pl.when(relays_on(c))
        def _():
            kv_copy(1, 1, c).wait_send()

        @pl.when(relays_back(c))
        def _():
            kv_copy(3, N_SEQ - 1, c).wait_send()

    def att_copy(c):
        return remote(
            att.at[pl.ds(c * CH, CH), pl.ds(0, KV)],
            att.at[pl.ds(c * CH, CH), pl.ds(KV, KV)],
            s_at.at[c],
            r_at.at[c],
            peer(1),
        )

    def rs_copy(c):
        return remote(rs_send.at[c], rs_recv.at[c], s_rs.at[c], r_rs.at[c], peer(2))

    def st_copy(c, k):
        return remote(st_send.at[c], st_recv.at[c, k - 1], s_st.at[c, k - 1], r_st.at[c, k - 1], peer(k))

    for c in range(NC):
        for h in range(2):
            z_copy(c, h).start()
    own_copy.start()
    sib_copy.start()
    for k in range(4):
        for cp in w_copies(k):
            cp.start()
    for cp in wo_copies + wo_remote:
        cp.start()

    acc[...] = jnp.zeros_like(acc)
    ss[...] = jnp.zeros_like(ss)
    o_acc[...] = jnp.zeros_like(o_acc)
    l_acc[...] = jnp.zeros_like(l_acc)
    for k in (1, 2, 3):
        @pl.when(seq < k)
        def _():
            for c in range(1 if k == 3 else 0, NC):
                kvb[c, pl.ds((3 - k) * CH, CH), :] = jnp.zeros((CH, KV), BF16)

    gi_row = gi[...].reshape(1, WIDTH)
    for i in range(8):
        gtab[i] = jnp.broadcast_to(gi_row[:, i * HALF : (i + 1) * HALF], (8, HALF))

    lane = lax.broadcasted_iota(jnp.int32, (CH, CH), 1)
    sub = lax.broadcasted_iota(jnp.int32, (CH, CH), 0)
    half_lane = jnp.where(lane >= 64, lane - 64, lane).astype(F32)
    inverse_freq = jnp.exp(half_lane * (-math.log(10000.0) / 64))
    for c in range(NC):
        p_row = pos[pl.ds(c * CH, CH)].reshape(1, CH).astype(F32)
        p_mat = jnp.broadcast_to(p_row, (CH, CH)).T
        angle = p_mat * inverse_freq
        sine = jnp.sin(angle)
        rope_c[c] = jnp.cos(angle)
        rope_s[c] = jnp.where(lane < 64, -sine, sine)
        i_rel = sub + c * CH
        low = i_rel - jnp.minimum(p_mat.astype(jnp.int32), 1023)
        for cc in range(NC):
            first = 3 if cc > c else 2
            for n in range(3):
                j_rel = CH * cc + ROWS * (n - first) + lane
                bias[c, cc, :, pl.ds(n * CH, CH)] = jnp.where((j_rel >= low) & (j_rel <= i_rel), 0.0, -1e30)

    own_copy.wait()
    for c in range(NC):
        x = xg[0, :, pl.ds(c * CH, CH)].astype(F32).T
        x = jnp.concatenate([x, jnp.zeros((CH, PAD - OWN), F32)], axis=1)
        tok[pl.ds(c * CH, CH), :] = jnp.where(core == 1, pltpu.roll(x, 64, 1), x)

    def step(k, c, h):
        cols = pl.ds(pl.multiple_of(c * CH, CH), CH)
        feats = pl.ds(pl.multiple_of(h * HALF, 16), HALF)
        x = xg[k, feats, cols].astype(F32)
        ss[c] += jnp.broadcast_to(jnp.sum(x * x, axis=0, keepdims=True), (8, CH))
        gain = gtab[tp_of(k) * 2 + h, pl.ds(0, 1), :]
        x = (x.T * gain).astype(BF16)
        acc[cols, pl.ds(0, 768)] += jnp.dot(x, wqv[k, feats, :], preferred_element_type=F32)
        acc[cols, pl.ds(768, 384)] += jnp.dot(x, wkv[k, feats, :], preferred_element_type=F32)
        acc[cols, pl.ds(1152, 384)] += jnp.dot(x, wvv[k, feats, :], preferred_element_type=F32)

    def local_steps(k):
        for cp in w_copies(k):
            cp.wait()

        @pl.loop(0, NC * 2)
        def _(i):
            step(k, i // 2, lax.rem(i, 2))

    local_steps(0)
    sib_copy.wait_recv()
    local_steps(1)
    for k in (2, 3):
        for cp in w_copies(k):
            cp.wait()

    def head(u, gain, c):
        mean = jnp.mean(u * u, axis=-1, keepdims=True)
        u = u * lax.rsqrt(mean + EPS) * gain
        return (u * rope_c[c] + pltpu.roll(u, 64, 1) * rope_s[c]).astype(BF16)

    def finish(c):
        rows = pl.ds(c * CH, CH)
        mean = ss[c, pl.ds(0, 1), :] / WIDTH
        scale = jnp.broadcast_to(lax.rsqrt(mean + EPS), (CH, CH)).T
        for h in range(3):
            u = acc[rows, pl.ds(768 + h * 128, 128)] * scale
            kvb[c, pl.ds(3 * CH, CH), pl.ds(h * 128, 128)] = head(u, gk[...].reshape(1, 128), c)
            v = acc[rows, pl.ds(1152 + h * 128, 128)] * scale
            kvb[c, pl.ds(3 * CH, CH), pl.ds(384 + h * 128, 128)] = v.astype(BF16)

    def finish_q(c):
        rows = pl.ds(c * CH, CH)
        mean = ss[c, pl.ds(0, 1), :] / WIDTH
        scale = jnp.broadcast_to(lax.rsqrt(mean + EPS), (CH, CH)).T
        for h in range(3):
            for g in range(2):
                u = acc[rows, pl.ds((2 * h + g) * 128, 128)] * scale
                qs[c, h, pl.ds(g * CH, CH), :] = head(u, gq[...].reshape(1, 128), c)

    for c in range(NC):
        @pl.loop(0, 2)
        def _(h):
            z_copy(c, h).wait_recv()
            f_copy(c, h).start()
            step(2, c, h)
            f_copy(c, h).wait_recv()
            step(3, c, h)

        finish(c)
        for ahead in (1, 3):
            send_kv(ahead, c)
            send_values(ahead, c)
            if c != 1:
                send_keys(ahead, c)
        if c == 1:
            relay_on(0, seq != 16)
        if c == 2:
            for ahead in (1, 3):
                send_keys(ahead, 1)
            for early in (0, 1):
                for ahead in (1, 3):
                    pass_values(ahead, early)
            relay_on(0, seq == 16)
            relay_back(0)
        finish_q(c)

    def unit(c, cc):
        start = 0 if cc > c else CH
        b = bias[c, cc]
        b = jnp.concatenate([b, b], axis=0)
        for h in range(3):
            keys = kvb[cc, pl.ds(start, 3 * CH), pl.ds(h * 128, 128)]
            vals = kvb[cc, pl.ds(start, 3 * CH), pl.ds(384 + h * 128, 128)]
            s = lax.dot_general(qs[c, h], keys, (((1,), (1,)), ((), ())), preferred_element_type=F32)
            w = jnp.exp2(s * SCORE + b)
            l_acc[c, h] += w[:, 0:128] + w[:, 128:256] + w[:, 256:384]
            o_acc[c, h] += jnp.dot(w.astype(BF16), vals, preferred_element_type=F32)

    relay_on(1)
    relay_back(1)
    kv_arrived(0)
    for c in range(NC):
        unit(c, 0)
    for ahead in (1, 3):
        pass_values(ahead, 2)
    relay_on(2)
    relay_back(2)
    kv_arrived(1)
    for c in range(NC):
        unit(c, 1)
    kv_arrived(2)
    for cp in wo_copies:
        cp.wait()
    for cp in wo_remote:
        cp.wait()

    def project(c, i):
        return jnp.dot(att[pl.ds(c * CH, CH), :], wov[i], preferred_element_type=F32)

    for c in range(NC):
        unit(c, 2)
        for h in range(3):
            total = jnp.sum(l_acc[c, h], axis=-1, keepdims=True)
            o = (o_acc[c, h] / total).astype(BF16)
            att[pl.ds(c * CH, CH), pl.ds(2 * h * 128, 128)] = o[:CH]
            att[pl.ds(c * CH, CH), pl.ds((2 * h + 1) * 128, 128)] = o[CH:]
        att_copy(c).start()
        if c > 0:
            att_copy(c - 1).wait_recv()
            rs_send[c - 1] = project(c - 1, 0).astype(BF16)
            rs_copy(c - 1).start()
    att_copy(2).wait_recv()
    rs_send[2] = project(2, 0).astype(BF16)
    rs_copy(2).start()

    for c in range(NC):
        own[pl.ds(c * CH, CH), :] = project(c, 1)

    gain_post = gpost[pl.ds(col_start(0), PAD)].reshape(1, PAD)
    gain_pre = gpre[pl.ds(col_start(0), PAD)].reshape(1, PAD)
    col = lax.broadcasted_iota(jnp.int32, (1, PAD), 1) - 64 * core
    inside = ((col >= 0) & (col < OWN)).astype(F32)

    def stats(c):
        rows = pl.ds(c * CH, CH)
        rs_copy(c).wait_recv()
        s = (own[rows, :] + rs_recv[c].astype(F32)) * inside
        own[rows, :] = s
        t = tok[rows, :]
        sg = s * gain_post
        both = [jnp.sum(v, axis=-1, keepdims=True) for v in (s * s, t * t, t * sg, sg * sg)]
        table = jnp.where(lane == 0, both[0], jnp.where(lane == 1, both[1], jnp.where(lane == 2, both[2], both[3])))
        st_send[c] = table.T[0:8, :]
        for k in (1, 2, 3):
            st_copy(c, k).start()

    def final(c):
        rows = pl.ds(c * CH, CH)
        for k in (1, 2, 3):
            st_copy(c, k).wait_recv()
        rows4 = st_send[c] + st_recv[c, 0] + st_recv[c, 1] + st_recv[c, 2]
        post = lax.rsqrt(rows4[0:1] / WIDTH + EPS)
        square = rows4[1:2] + 2.0 * post * rows4[2:3] + post * post * rows4[3:4]
        pre = lax.rsqrt(jnp.maximum(square, 0.0) / WIDTH + EPS)
        post = jnp.broadcast_to(post, (CH, CH)).T[:, 0:1]
        pre = jnp.broadcast_to(pre, (CH, CH)).T[:, 0:1]
        hidden = (tok[rows, :] + own[rows, :] * post * gain_post).astype(BF16).astype(F32)
        out = hidden * pre * gain_pre

        def place(v):
            return jnp.where(core == 1, pltpu.roll(v, PAD - 64, 1), v)[:, :OWN].T.astype(BF16)

        hid[:, rows] = place(hidden)
        ffn[:, rows] = place(out)

    for c in range(NC):
        stats(c)
        final(c)

    sib_copy.wait_send()
    for c in range(NC):
        for h in range(2):
            z_copy(c, h).wait_send()
            f_copy(c, h).wait_send()
        for k in (1, 2, 3):
            st_copy(c, k).wait_send()

        kv_left(c)
        att_copy(c).wait_send()
        rs_copy(c).wait_send()


def local(tokens, positions, w_query, w_key, w_value, w_out, gain_input, gain_query, gain_key, gain_post, gain_pre):
    hbm = pl.BlockSpec(memory_space=pltpu.MemorySpace.HBM)
    vmem = pl.BlockSpec(memory_space=pltpu.VMEM)
    dma = pltpu.SemaphoreType.DMA
    out = jax.ShapeDtypeStruct((OWN, ROWS), BF16)
    hidden, ffn_input = pl.pallas_call(
        kernel,
        out_shape=(out, out),
        in_specs=[hbm, vmem, hbm, hbm, hbm, hbm, vmem, vmem, vmem, vmem, vmem],
        out_specs=(vmem, vmem),
        scratch_shapes=[
            pltpu.VMEM((4, OWN, ROWS), BF16),
            pltpu.VMEM((4, OWN, 768), BF16),
            pltpu.VMEM((4, OWN, 384), BF16),
            pltpu.VMEM((4, OWN, 384), BF16),
            pltpu.VMEM((2, 2 * KV, PAD), BF16),
            pltpu.VMEM((ROWS, 1536), F32),
            pltpu.VMEM((NC, 8, CH), F32),
            pltpu.VMEM((8, 8, HALF), F32),
            pltpu.VMEM((NC, CH, CH), F32),
            pltpu.VMEM((NC, CH, CH), F32),
            pltpu.VMEM((NC, NC, CH, 3 * CH), F32),
            pltpu.VMEM((NC, 3, 2 * CH, 128), BF16),
            pltpu.VMEM((NC, 4 * CH, KV), BF16),
            pltpu.VMEM((NC, 3, 2 * CH, 128), F32),
            pltpu.VMEM((NC, 3, 2 * CH, 128), F32),
            pltpu.VMEM((ROWS, 2 * KV), BF16),
            pltpu.VMEM((NC, CH, PAD), BF16),
            pltpu.VMEM((NC, CH, PAD), BF16),
            pltpu.VMEM((ROWS, PAD), F32),
            pltpu.VMEM((ROWS, PAD), F32),
            pltpu.VMEM((NC, 8, CH), F32),
            pltpu.VMEM((NC, 3, 8, CH), F32),
            pltpu.VMEM((2, NC, CH, 384), BF16),
            dma, dma, dma,
            dma((NC, 2)), dma((NC, 2)), dma((NC, 2)), dma((NC, 2)),
            dma((3, 4)), dma((2,)), dma((2,)), dma((2,)),
            dma((4, NC)), dma((3, NC)),
            dma((2, NC)), dma((2, NC)), dma((2, NC)), dma((2, NC)),
            dma((NC,)), dma((NC,)), dma((NC,)), dma((NC,)),
            dma((NC, 3)), dma((NC, 3)),
        ],
        compiler_params=pltpu.CompilerParams(
            collective_id=0, has_side_effects=True, vmem_limit_bytes=60 * 1024 * 1024
        ),
        cost_estimate=pl.CostEstimate(flops=12_000_000_000, bytes_accessed=28_000_000, transcendentals=3_000_000),
    )(
        tokens.T,
        positions,
        w_query,
        w_key,
        w_value,
        w_out,
        gain_input,
        gain_query,
        gain_key,
        gain_post,
        gain_pre,
    )
    return hidden.T, ffn_input.T


def solution(mesh):
    torus = Mesh(mesh.devices.reshape(N_SEQ, 2, 2), ("seq", "tp_0", "tp_1"))
    tp = ("tp_0", "tp_1")
    return jax.shard_map(
        local,
        mesh=torus,
        in_specs=(
            P("seq", tp), P("seq"), P(None, tp), P(None, tp), P(None, tp), P(tp, None),
            P(), P(), P(), P(), P(),
        ),
        out_specs=(P("seq", tp), P("seq", tp)),
        check_vma=False,
    )
```

```python
import functools
import math

import jax
import jax.numpy as jnp
from jax import lax
from jax.experimental import pallas as pl
from jax.experimental.pallas import tpu as pltpu
from jax.sharding import Mesh
from jax.sharding import PartitionSpec as P

F32 = jnp.float32
BF16 = jnp.bfloat16
MESH = pl.DeviceIdType.MESH

EPS = 1e-6
WIDTH = 5376
PARTS = 4
OWN = 1344
HALF = 672
PAD = 1408
ROWS = 384
CH = 128
NC = 3
KV = 768
N_SEQ = 32
SCORE = 168.0**-0.5 * math.log2(math.e)


def kernel(
    xt, pos, wq, wk, wv, wo, gi, gq, gk, gpost, gpre,
    hid, ffn,
    xg, wqv, wkv, wvv, wov, acc, ss, gtab, rope_c, rope_s, bias,
    qs, kvb, o_acc, l_acc, att, rs_send, rs_recv, own, post_t, pre_t, turned, hid_v, ffn_v, st_send, st_recv, stage,
    s_own, s_sib, r_sib, s_z, r_z, s_f, r_f, s_w, s_wo, s_wos, r_wos,
    s_kv, r_kv, s_stage, r_stage, s_pass, r_pass, s_at, r_at, s_rs, r_rs, s_st, r_st, s_out,
):
    seq = lax.axis_index("seq")
    zl = lax.axis_index("tp_0")
    core = lax.axis_index("tp_1")

    def peer(k):
        return (seq, lax.rem(zl + k // 2, 2), lax.rem(core + k % 2, 2))

    def tp_of(k):
        return lax.rem(zl + k // 2, 2) * 2 + lax.rem(core + k % 2, 2)

    def col_start(k):
        t = tp_of(k)
        return pl.multiple_of(OWN * t - 64 * lax.rem(t, 2), 128)

    def later(k, dz=0):
        return (lax.rem(seq + k, N_SEQ), lax.rem(zl + dz, 2), core)

    barrier = pltpu.get_barrier_semaphore()
    halves = jnp.where((seq >= 13) & (seq < 19), 1, 0) + jnp.where((seq == 15) | (seq == 16), 1, 0)
    partners = 3 + halves
    for k in (1, 2, 3):
        pl.semaphore_signal(barrier, inc=1, device_id=peer(k), device_id_type=MESH)
    for k in (1, 3):
        for there, step_to in ((seq + k < N_SEQ, k), (seq >= k, N_SEQ - k)):
            partners += jnp.where(there, 1, 0)

            @pl.when(there)
            def _():
                pl.semaphore_signal(barrier, inc=1, device_id=later(step_to), device_id_type=MESH)

    for there, step_to in (
        ((seq >= 13) & (seq < 16), 3),
        ((seq >= 16) & (seq < 19), N_SEQ - 3),
        (seq == 15, 1),
        (seq == 16, N_SEQ - 1),
    ):
        @pl.when(there)
        def _():
            pl.semaphore_signal(barrier, inc=1, device_id=later(step_to, 1), device_id_type=MESH)

    def remote(src, dst, ss_, rs_, dev):
        return pltpu.make_async_remote_copy(
            src_ref=src, dst_ref=dst, send_sem=ss_, recv_sem=rs_, device_id=dev, device_id_type=MESH
        )

    def piece(ref, c, h):
        return ref.at[pl.ds(h * HALF, HALF), pl.ds(c * CH, CH)]

    def z_copy(c, h):
        return remote(piece(xt, c, h), piece(xg.at[2], c, h), s_z.at[c, h], r_z.at[c, h], peer(2))

    def f_copy(c, h):
        return remote(piece(xg.at[2], c, h), piece(xg.at[3], c, h), s_f.at[c, h], r_f.at[c, h], peer(1))

    sib_copy = remote(xt, xg.at[1], s_sib, r_sib, peer(1))
    own_copy = pltpu.make_async_copy(xt, xg.at[0], s_own)

    def w_copies(k):
        first = pl.multiple_of(tp_of(k) * OWN, 16)
        return [
            pltpu.make_async_copy(a.at[pl.ds(first, OWN)], b.at[k], s_w.at[i, k])
            for i, (a, b) in enumerate(((wq, wqv), (wk, wkv), (wv, wvv)))
        ]

    wo_copies = [
        pltpu.make_async_copy(wo.at[:, pl.ds(col_start(k), PAD)], wov.at[i, pl.ds(0, KV)], s_wo.at[i])
        for i, k in enumerate((2, 0))
    ]
    wo_remote = [
        remote(wo.at[:, pl.ds(col_start(k), PAD)], wov.at[i, pl.ds(KV, KV)], s_wos.at[i], r_wos.at[i], peer(1))
        for i, k in enumerate((3, 1))
    ]

    def kv_copy(back, ahead, c):
        far = (back + ahead) % N_SEQ
        return remote(
            kvb.at[c, pl.ds((3 - back) * CH, CH)],
            kvb.at[c, pl.ds((3 - far) * CH, CH)],
            s_kv.at[3 if back == 3 else far - 1, c],
            r_kv.at[far - 1, c],
            later(ahead),
        )

    seq16 = lax.rem(seq, 16)
    crossing = (seq16 >= 13) & (seq < 16)

    def key_copy(ahead, c):
        return remote(
            kvb.at[c, pl.ds(3 * CH, CH), pl.ds(0, 384)],
            kvb.at[c, pl.ds((3 - ahead) * CH, CH), pl.ds(0, 384)],
            s_kv.at[ahead - 1, c],
            r_kv.at[ahead - 1, c],
            later(ahead),
        )

    def value_copy(ahead, c):
        return remote(
            kvb.at[c, pl.ds(3 * CH, CH), pl.ds(384, 384)],
            stage.at[ahead // 2, c],
            s_stage.at[ahead // 2, c],
            r_stage.at[ahead // 2, c],
            later(ahead, 1),
        )

    def value_pass(ahead, c):
        return remote(
            stage.at[ahead // 2, c],
            kvb.at[c, pl.ds((3 - ahead) * CH, CH), pl.ds(384, 384)],
            s_pass.at[ahead // 2, c],
            r_pass.at[ahead // 2, c],
            peer(2),
        )

    def sends(ahead, c):
        if ahead == 3 and c == 0:
            return seq == 14
        return seq < N_SEQ - ahead

    def crosses(ahead, c):
        if ahead == 1:
            return seq == 15
        return (seq == 14) if c == 0 else crossing

    def crossed(ahead, c):
        if ahead == 1:
            return seq == 16
        return (seq == 17) if c == 0 else (seq >= 16) & (seq < 19)

    def relays_on(c):
        on = (seq >= 1) & (seq < N_SEQ - 1)
        return on & (seq != 15) if c == 0 else on & (seq16 == 14)

    def relays_back(c):
        return (seq == 17) if c == 0 else (seq >= 3) & (seq16 != 0)

    def send_kv(ahead, c):
        @pl.when(sends(ahead, c) & jnp.logical_not(crosses(ahead, c)))
        def _():
            kv_copy(0, ahead, c).start()

    def send_values(ahead, c):
        @pl.when(crosses(ahead, c))
        def _():
            value_copy(ahead, c).start()

    def send_keys(ahead, c):
        @pl.when(crosses(ahead, c))
        def _():
            key_copy(ahead, c).start()

    def pass_values(ahead, c):
        @pl.when(crossed(ahead, c))
        def _():
            value_copy(ahead, c).wait_recv()
            value_pass(ahead, c).start()

    def got_kv(ahead, c, other):
        @pl.when(other & crossed(ahead, c))
        def _():
            key_copy(ahead, c).wait_recv()
            value_pass(ahead, c).wait_recv()

        first = (seq >= 1) if ahead == 1 else (seq >= 3) if c > 0 else (seq < 0)

        @pl.when(other & first & jnp.logical_not(crossed(ahead, c)))
        def _():
            kv_copy(0, ahead, c).wait_recv()

    def relay_on(c, some=True):
        got_kv(1, c, relays_on(c) & some)

        @pl.when(relays_on(c) & some)
        def _():
            kv_copy(1, 1, c).start()

    def relay_back(c):
        got_kv(3, c, relays_back(c))

        @pl.when(relays_back(c))
        def _():
            kv_copy(3, N_SEQ - 1, c).start()

    def kv_arrived(c):
        got_kv(1, c, jnp.logical_not(relays_on(c)))

        @pl.when(seq >= 2)
        def _():
            kv_copy(1, 1, c).wait_recv()

        got_kv(3, c, jnp.logical_not(relays_back(c)))

    def kv_left(c):
        for ahead in (1, 3):
            @pl.when(sends(ahead, c) & jnp.logical_not(crosses(ahead, c)))
            def _():
                kv_copy(0, ahead, c).wait_send()

            @pl.when(crosses(ahead, c))
            def _():
                value_copy(ahead, c).wait_send()
                key_copy(ahead, c).wait_send()

            @pl.when(crossed(ahead, c))
            def _():
                value_pass(ahead, c).wait_send()

        @pl.when(relays_on(c))
        def _():
            kv_copy(1, 1, c).wait_send()

        @pl.when(relays_back(c))
        def _():
            kv_copy(3, N_SEQ - 1, c).wait_send()

    def att_copy(c):
        return remote(
            att.at[pl.ds(c * CH, CH), pl.ds(0, KV)],
            att.at[pl.ds(c * CH, CH), pl.ds(KV, KV)],
            s_at.at[c],
            r_at.at[c],
            peer(1),
        )

    def rs_copy(c):
        return remote(rs_send.at[c], rs_recv.at[c], s_rs.at[c], r_rs.at[c], peer(2))

    def st_copy(c, k):
        return remote(st_send.at[c], st_recv.at[c, k - 1], s_st.at[c, k - 1], r_st.at[c, k - 1], peer(k))

    own_copy.start()
    for k in range(2):
        for cp in w_copies(k):
            cp.start()
    pl.semaphore_wait(barrier, partners)
    for c in range(NC):
        for h in range(2):
            z_copy(c, h).start()
    sib_copy.start()
    for k in (2, 3):
        for cp in w_copies(k):
            cp.start()
    for cp in wo_copies + wo_remote:
        cp.start()

    acc[...] = jnp.zeros_like(acc)
    ss[...] = jnp.zeros_like(ss)
    o_acc[...] = jnp.zeros_like(o_acc)
    l_acc[...] = jnp.zeros_like(l_acc)
    for k in (1, 2, 3):
        @pl.when(seq < k)
        def _():
            for c in range(1 if k == 3 else 0, NC):
                kvb[c, pl.ds((3 - k) * CH, CH), :] = jnp.zeros((CH, KV), BF16)

    gi_row = gi[...].reshape(1, WIDTH)
    for i in range(8):
        gtab[i] = jnp.broadcast_to(gi_row[:, i * HALF : (i + 1) * HALF], (8, HALF))

    lane = lax.broadcasted_iota(jnp.int32, (CH, CH), 1)
    sub = lax.broadcasted_iota(jnp.int32, (CH, CH), 0)
    half_lane = jnp.where(lane >= 64, lane - 64, lane).astype(F32)
    inverse_freq = jnp.exp(half_lane * (-math.log(10000.0) / 64))
    for c in range(NC):
        p_row = pos[pl.ds(c * CH, CH)].reshape(1, CH).astype(F32)
        p_mat = jnp.broadcast_to(p_row, (CH, CH)).T
        angle = p_mat * inverse_freq
        sine = jnp.sin(angle)
        rope_c[c] = jnp.cos(angle)
        rope_s[c] = jnp.where(lane < 64, -sine, sine)
        i_rel = sub + c * CH
        low = i_rel - jnp.minimum(p_mat.astype(jnp.int32), 1023)
        for cc in range(NC):
            first = 3 if cc > c else 2
            for n in range(3):
                j_rel = CH * cc + ROWS * (n - first) + lane
                bias[c, cc, :, pl.ds(n * CH, CH)] = jnp.where((j_rel >= low) & (j_rel <= i_rel), 0.0, -1e30)

    def own_rows(wide):
        turned[...] = wide.T
        return turned.at[pl.ds(pl.multiple_of(64 * core, 64), OWN)]

    for gain, table in ((gpost, post_t), (gpre, pre_t)):
        row = gain[pl.ds(col_start(0), PAD)].reshape(1, PAD)
        table[...] = own_rows(jnp.broadcast_to(row, (CH, PAD)))[...]

    own_copy.wait()

    def step(k, c, h):
        cols = pl.ds(pl.multiple_of(c * CH, CH), CH)
        feats = pl.ds(pl.multiple_of(h * HALF, 16), HALF)
        x = xg[k, feats, cols].astype(F32)
        ss[c] += jnp.broadcast_to(jnp.sum(x * x, axis=0, keepdims=True), (8, CH))
        gain = gtab[tp_of(k) * 2 + h, pl.ds(0, 1), :]
        x = (x.T * gain).astype(BF16)
        acc[cols, pl.ds(0, 768)] += jnp.dot(x, wqv[k, feats, :], preferred_element_type=F32)
        acc[cols, pl.ds(768, 384)] += jnp.dot(x, wkv[k, feats, :], preferred_element_type=F32)
        acc[cols, pl.ds(1152, 384)] += jnp.dot(x, wvv[k, feats, :], preferred_element_type=F32)

    def local_steps(k):
        for cp in w_copies(k):
            cp.wait()

        @pl.loop(0, NC * 2)
        def _(i):
            step(k, i // 2, lax.rem(i, 2))

    local_steps(0)
    sib_copy.wait_recv()
    local_steps(1)
    for k in (2, 3):
        for cp in w_copies(k):
            cp.wait()

    def head(u, gain, c):
        mean = jnp.mean(u * u, axis=-1, keepdims=True)
        u = u * lax.rsqrt(mean + EPS) * gain
        return (u * rope_c[c] + pltpu.roll(u, 64, 1) * rope_s[c]).astype(BF16)

    def finish(c):
        rows = pl.ds(c * CH, CH)
        mean = ss[c, pl.ds(0, 1), :] / WIDTH
        scale = jnp.broadcast_to(lax.rsqrt(mean + EPS), (CH, CH)).T
        for h in range(3):
            u = acc[rows, pl.ds(768 + h * 128, 128)] * scale
            kvb[c, pl.ds(3 * CH, CH), pl.ds(h * 128, 128)] = head(u, gk[...].reshape(1, 128), c)
            v = acc[rows, pl.ds(1152 + h * 128, 128)] * scale
            kvb[c, pl.ds(3 * CH, CH), pl.ds(384 + h * 128, 128)] = v.astype(BF16)

    def finish_q(c):
        rows = pl.ds(c * CH, CH)
        mean = ss[c, pl.ds(0, 1), :] / WIDTH
        scale = jnp.broadcast_to(lax.rsqrt(mean + EPS), (CH, CH)).T
        for h in range(3):
            for g in range(2):
                u = acc[rows, pl.ds((2 * h + g) * 128, 128)] * scale
                qs[c, h, pl.ds(g * CH, CH), :] = head(u, gq[...].reshape(1, 128), c)

    for c in range(NC):
        @pl.loop(0, 2)
        def _(h):
            z_copy(c, h).wait_recv()
            f_copy(c, h).start()
            step(2, c, h)
            f_copy(c, h).wait_recv()
            step(3, c, h)

        finish(c)
        for ahead in (1, 3):
            send_kv(ahead, c)
            send_values(ahead, c)
            if c != 1:
                send_keys(ahead, c)
        if c == 1:
            relay_on(0, seq != 16)
        if c == 2:
            for ahead in (1, 3):
                send_keys(ahead, 1)
            for early in (0, 1):
                for ahead in (1, 3):
                    pass_values(ahead, early)
            relay_on(0, seq == 16)
            relay_back(0)
        finish_q(c)

    def unit(c, cc):
        start = 0 if cc > c else CH
        b = bias[c, cc]
        b = jnp.concatenate([b, b], axis=0)
        for h in range(3):
            keys = kvb[cc, pl.ds(start, 3 * CH), pl.ds(h * 128, 128)]
            vals = kvb[cc, pl.ds(start, 3 * CH), pl.ds(384 + h * 128, 128)]
            s = lax.dot_general(qs[c, h], keys, (((1,), (1,)), ((), ())), preferred_element_type=F32)
            w = jnp.exp2(s * SCORE + b)
            l_acc[c, h] += w[:, 0:128] + w[:, 128:256] + w[:, 256:384]
            o_acc[c, h] += jnp.dot(w.astype(BF16), vals, preferred_element_type=F32)

    relay_on(1)
    relay_back(1)
    kv_arrived(0)
    for c in range(NC):
        unit(c, 0)
    for ahead in (1, 3):
        pass_values(ahead, 2)
    relay_on(2)
    relay_back(2)
    kv_arrived(1)
    for c in range(NC):
        unit(c, 1)
    kv_arrived(2)
    for cp in wo_copies:
        cp.wait()
    for cp in wo_remote:
        cp.wait()

    def project(c, i):
        return jnp.dot(att[pl.ds(c * CH, CH), :], wov[i], preferred_element_type=F32)

    for c in range(NC):
        unit(c, 2)
        for h in range(3):
            total = jnp.sum(l_acc[c, h], axis=-1, keepdims=True)
            o = (o_acc[c, h] / total).astype(BF16)
            att[pl.ds(c * CH, CH), pl.ds(2 * h * 128, 128)] = o[:CH]
            att[pl.ds(c * CH, CH), pl.ds((2 * h + 1) * 128, 128)] = o[CH:]
        att_copy(c).start()
        if c > 0:
            att_copy(c - 1).wait_recv()
            rs_send[c - 1] = own_rows(project(c - 1, 0))[...].astype(BF16)
            rs_copy(c - 1).start()
    att_copy(2).wait_recv()
    rs_send[2] = own_rows(project(2, 0))[...].astype(BF16)
    rs_copy(2).start()

    for c in range(NC):
        own[c] = own_rows(project(c, 1))[...]

    BLOCK = 64

    def stats(c):
        cols = pl.ds(c * CH, CH)
        rs_copy(c).wait_recv()

        def one(i, sums):
            rows = pl.ds(pl.multiple_of(i * BLOCK, BLOCK), BLOCK)
            s = own[c, rows, :] + rs_recv[c, rows, :].astype(F32)
            t = xg[0, rows, cols].astype(F32)
            sg = s * post_t[rows, :]
            own[c, rows, :] = s
            return tuple(
                a + jnp.sum((u * v).reshape(BLOCK // 8, 8, CH), axis=0)
                for a, u, v in zip(sums, (s, t, t, sg), (s, t, sg, sg))
            )

        sums = lax.fori_loop(0, OWN // BLOCK, one, (jnp.zeros((8, CH), F32),) * 4)
        for i, v in enumerate(sums):
            st_send[c, pl.ds(i, 1), :] = jnp.sum(v, axis=0, keepdims=True)
        for i in range(4, 8):
            st_send[c, pl.ds(i, 1), :] = jnp.zeros((1, CH), F32)
        for k in (1, 2, 3):
            st_copy(c, k).start()

    def final(c):
        cols = pl.ds(c * CH, CH)
        for k in (1, 2, 3):
            st_copy(c, k).wait_recv()
        rows4 = st_send[c] + st_recv[c, 0] + st_recv[c, 1] + st_recv[c, 2]
        post = lax.rsqrt(rows4[0:1] / WIDTH + EPS)
        square = rows4[1:2] + 2.0 * post * rows4[2:3] + post * post * rows4[3:4]
        pre = lax.rsqrt(jnp.maximum(square, 0.0) / WIDTH + EPS)

        @pl.loop(0, OWN // BLOCK)
        def _(i):
            rows = pl.ds(pl.multiple_of(i * BLOCK, BLOCK), BLOCK)
            t = xg[0, rows, cols].astype(F32)
            hidden = (t + own[c, rows, :] * post * post_t[rows, :]).astype(BF16)
            hid_v[rows, cols] = hidden
            ffn_v[rows, cols] = (hidden.astype(F32) * pre * pre_t[rows, :]).astype(BF16)

        for cp in out_copies(c):
            cp.start()

    def out_copies(c):
        cols = pl.ds(c * CH, CH)
        return [
            pltpu.make_async_copy(hid_v.at[:, cols], hid.at[:, cols], s_out.at[0, c]),
            pltpu.make_async_copy(ffn_v.at[:, cols], ffn.at[:, cols], s_out.at[1, c]),
        ]

    for c in range(NC):
        stats(c)
        if c > 0:
            final(c - 1)
    final(NC - 1)

    sib_copy.wait_send()
    for c in range(NC):
        for h in range(2):
            z_copy(c, h).wait_send()
            f_copy(c, h).wait_send()
        for k in (1, 2, 3):
            st_copy(c, k).wait_send()

        kv_left(c)
        att_copy(c).wait_send()
        rs_copy(c).wait_send()
        for cp in out_copies(c):
            cp.wait()


def copy_out(hidden, ffn_input, hid, ffn, buf, sem_in, sem_out):
    part = OWN // PARTS
    pieces = [
        (
            pltpu.make_async_copy(a.at[pl.ds(i * part, part)], buf.at[n, pl.ds(i * part, part)], sem_in.at[n, i]),
            pltpu.make_async_copy(buf.at[n, pl.ds(i * part, part)], b.at[pl.ds(i * part, part)], sem_out.at[n, i]),
        )
        for n, (a, b) in enumerate(((hidden, hid), (ffn_input, ffn)))
        for i in range(PARTS)
    ]
    for into, _ in pieces:
        into.start()
    for into, away in pieces:
        into.wait()
        away.start()
    for _, away in pieces:
        away.wait()


def local(tokens, positions, w_query, w_key, w_value, w_out, gain_input, gain_query, gain_key, gain_post, gain_pre):
    hbm = pl.BlockSpec(memory_space=pltpu.MemorySpace.HBM)
    vmem = pl.BlockSpec(memory_space=pltpu.VMEM)
    dma = pltpu.SemaphoreType.DMA
    out = jax.ShapeDtypeStruct((OWN, ROWS), BF16)
    hidden, ffn_input = pl.pallas_call(
        kernel,
        out_shape=(out, out),
        in_specs=[hbm, vmem, hbm, hbm, hbm, hbm, vmem, vmem, vmem, vmem, vmem],
        out_specs=(hbm, hbm),
        scratch_shapes=[
            pltpu.VMEM((4, OWN, ROWS), BF16),
            pltpu.VMEM((4, OWN, 768), BF16),
            pltpu.VMEM((4, OWN, 384), BF16),
            pltpu.VMEM((4, OWN, 384), BF16),
            pltpu.VMEM((2, 2 * KV, PAD), BF16),
            pltpu.VMEM((ROWS, 1536), F32),
            pltpu.VMEM((NC, 8, CH), F32),
            pltpu.VMEM((8, 8, HALF), F32),
            pltpu.VMEM((NC, CH, CH), F32),
            pltpu.VMEM((NC, CH, CH), F32),
            pltpu.VMEM((NC, NC, CH, 3 * CH), F32),
            pltpu.VMEM((NC, 3, 2 * CH, 128), BF16),
            pltpu.VMEM((NC, 4 * CH, KV), BF16),
            pltpu.VMEM((NC, 3, 2 * CH, 128), F32),
            pltpu.VMEM((NC, 3, 2 * CH, 128), F32),
            pltpu.VMEM((ROWS, 2 * KV), BF16),
            pltpu.VMEM((NC, OWN, CH), BF16),
            pltpu.VMEM((NC, OWN, CH), BF16),
            pltpu.VMEM((NC, OWN, CH), F32),
            pltpu.VMEM((OWN, CH), F32),
            pltpu.VMEM((OWN, CH), F32),
            pltpu.VMEM((PAD, CH), F32),
            pltpu.VMEM((OWN, ROWS), BF16),
            pltpu.VMEM((OWN, ROWS), BF16),
            pltpu.VMEM((NC, 8, CH), F32),
            pltpu.VMEM((NC, 3, 8, CH), F32),
            pltpu.VMEM((2, NC, CH, 384), BF16),
            dma, dma, dma,
            dma((NC, 2)), dma((NC, 2)), dma((NC, 2)), dma((NC, 2)),
            dma((3, 4)), dma((2,)), dma((2,)), dma((2,)),
            dma((4, NC)), dma((3, NC)),
            dma((2, NC)), dma((2, NC)), dma((2, NC)), dma((2, NC)),
            dma((NC,)), dma((NC,)), dma((NC,)), dma((NC,)),
            dma((NC, 3)), dma((NC, 3)), dma((2, NC)),
        ],
        compiler_params=pltpu.CompilerParams(
            collective_id=0, has_side_effects=True, vmem_limit_bytes=60 * 1024 * 1024
        ),
        cost_estimate=pl.CostEstimate(flops=12_000_000_000, bytes_accessed=28_000_000, transcendentals=3_000_000),
    )(
        tokens.T,
        positions,
        w_query,
        w_key,
        w_value,
        w_out,
        gain_input,
        gain_query,
        gain_key,
        gain_post,
        gain_pre,
    )
    copied = pl.pallas_call(
        copy_out,
        out_shape=(out, out),
        in_specs=[hbm, hbm],
        out_specs=(hbm, hbm),
        scratch_shapes=[pltpu.VMEM((2, OWN, ROWS), BF16), dma((2, PARTS)), dma((2, PARTS))],
        compiler_params=pltpu.CompilerParams(has_side_effects=True),
    )(hidden, ffn_input)
    return copied[0].T, copied[1].T


def solution(mesh):
    torus = Mesh(mesh.devices.reshape(N_SEQ, 2, 2), ("seq", "tp_0", "tp_1"))
    tp = ("tp_0", "tp_1")
    return jax.shard_map(
        local,
        mesh=torus,
        in_specs=(
            P("seq", tp), P("seq"), P(None, tp), P(None, tp), P(None, tp), P(tp, None),
            P(), P(), P(), P(), P(),
        ),
        out_specs=(P("seq", tp), P("seq", tp)),
        check_vma=False,
    )
```

```python
import functools
import math

import jax
import jax.numpy as jnp
from jax import lax
from jax.experimental import pallas as pl
from jax.experimental.pallas import tpu as pltpu
from jax.sharding import Mesh
from jax.sharding import PartitionSpec as P

F32 = jnp.float32
BF16 = jnp.bfloat16
MESH = pl.DeviceIdType.MESH

EPS = 1e-6
WIDTH = 5376
PARTS = 4
OWN = 1344
HALF = 672
PAD = 1408
ROWS = 384
CH = 128
NC = 3
KV = 768
N_SEQ = 32
SCORE = 168.0**-0.5 * math.log2(math.e)


def kernel(
    xt, pos, wq, wk, wv, wo, gi, gq, gk, gpost, gpre,
    hid, ffn,
    xg, wqv, wkv, wvv, wov, acc, ss, gtab, rope_c, rope_s, bias,
    qs, kvb, o_acc, l_acc, att, rs_send, rs_recv, own, post_t, pre_t, turned, hid_v, ffn_v, st_send, st_recv, stage,
    s_own, s_sib, r_sib, s_z, r_z, s_f, r_f, s_w, s_wo, s_wos, r_wos,
    s_kv, r_kv, s_stage, r_stage, s_pass, s_at, r_at, s_rs, r_rs, s_st, r_st, s_out,
):
    seq = lax.axis_index("seq")
    zl = lax.axis_index("tp_0")
    core = lax.axis_index("tp_1")

    def peer(k):
        return (seq, lax.rem(zl + k // 2, 2), lax.rem(core + k % 2, 2))

    def tp_of(k):
        return lax.rem(zl + k // 2, 2) * 2 + lax.rem(core + k % 2, 2)

    def col_start(k):
        t = tp_of(k)
        return pl.multiple_of(OWN * t - 64 * lax.rem(t, 2), 128)

    def later(k, dz=0):
        return (lax.rem(seq + k, N_SEQ), lax.rem(zl + dz, 2), core)

    barrier = pltpu.get_barrier_semaphore()
    halves = jnp.where((seq >= 13) & (seq < 19), 1, 0) + jnp.where((seq == 15) | (seq == 16), 1, 0)
    partners = 3 + halves
    for k in (1, 2, 3):
        pl.semaphore_signal(barrier, inc=1, device_id=peer(k), device_id_type=MESH)
    for k in (1, 3):
        for there, step_to in ((seq + k < N_SEQ, k), (seq >= k, N_SEQ - k)):
            partners += jnp.where(there, 1, 0)

            @pl.when(there)
            def _():
                pl.semaphore_signal(barrier, inc=1, device_id=later(step_to), device_id_type=MESH)

    for there, step_to in (
        ((seq >= 13) & (seq < 16), 3),
        ((seq >= 16) & (seq < 19), N_SEQ - 3),
        (seq == 15, 1),
        (seq == 16, N_SEQ - 1),
    ):
        @pl.when(there)
        def _():
            pl.semaphore_signal(barrier, inc=1, device_id=later(step_to, 1), device_id_type=MESH)

    def remote(src, dst, ss_, rs_, dev):
        return pltpu.make_async_remote_copy(
            src_ref=src, dst_ref=dst, send_sem=ss_, recv_sem=rs_, device_id=dev, device_id_type=MESH
        )

    def piece(ref, c, h):
        return ref.at[pl.ds(h * HALF, HALF), pl.ds(c * CH, CH)]

    def z_copy(c, h):
        return remote(piece(xt, c, h), piece(xg.at[2], c, h), s_z.at[c, h], r_z.at[c, h], peer(2))

    def f_copy(c, h):
        return remote(piece(xg.at[2], c, h), piece(xg.at[3], c, h), s_f.at[c, h], r_f.at[c, h], peer(1))

    sib_copy = remote(xt, xg.at[1], s_sib, r_sib, peer(1))
    own_copy = pltpu.make_async_copy(xt, xg.at[0], s_own)

    def w_copies(k):
        first = pl.multiple_of(tp_of(k) * OWN, 16)
        return [
            pltpu.make_async_copy(a.at[pl.ds(first, OWN)], b.at[k], s_w.at[i, k])
            for i, (a, b) in enumerate(((wq, wqv), (wk, wkv), (wv, wvv)))
        ]

    wo_copies = [
        pltpu.make_async_copy(wo.at[:, pl.ds(col_start(k), PAD)], wov.at[i, pl.ds(0, KV)], s_wo.at[i])
        for i, k in enumerate((2, 0))
    ]
    wo_remote = [
        remote(wo.at[:, pl.ds(col_start(k), PAD)], wov.at[i, pl.ds(KV, KV)], s_wos.at[i], r_wos.at[i], peer(1))
        for i, k in enumerate((3, 1))
    ]

    def kv_copy(back, ahead, c, part):
        far = (back + ahead) % N_SEQ
        cols = pl.ds(384 * part, 384)
        return remote(
            kvb.at[c, pl.ds((3 - back) * CH, CH), cols],
            kvb.at[c, pl.ds((3 - far) * CH, CH), cols],
            s_kv.at[3 if back == 3 else far - 1, c, part],
            r_kv.at[far - 1, c, part],
            later(ahead),
        )

    seq4 = lax.rem(seq, 4)
    seq16 = lax.rem(seq, 16)
    before_half = (seq >= 13) & (seq < 16)
    after_half = (seq >= 16) & (seq < 19)

    def value_copy(ahead, c):
        return remote(
            kvb.at[c, pl.ds(3 * CH, CH), pl.ds(384, 384)],
            stage.at[ahead // 2, c],
            s_stage.at[ahead // 2, c],
            r_stage.at[ahead // 2, c],
            later(ahead, 1),
        )

    def value_pass(ahead, c):
        return remote(
            stage.at[ahead // 2, c],
            kvb.at[c, pl.ds((3 - ahead) * CH, CH), pl.ds(384, 384)],
            s_pass.at[ahead // 2, c],
            r_kv.at[ahead - 1, c, 1],
            peer(2),
        )

    def sends(ahead, c):
        return (seq < N_SEQ - ahead) & (seq4 == 2) if ahead == 3 and c == 0 else seq < N_SEQ - ahead

    def gets(ahead, c):
        return (seq >= 3) & (seq4 == 1) if ahead == 3 and c == 0 else seq >= ahead

    def crosses(ahead, c):
        return seq == 15 if ahead == 1 else before_half & sends(3, c)

    def crossed(ahead, c):
        return seq == 16 if ahead == 1 else after_half & gets(3, c)

    def relays_on(c):
        on = (seq >= 1) & (seq < N_SEQ - 1)
        return on & (seq4 != 3) if c == 0 else on & (seq16 == 14)

    def relays_back(c):
        return (seq >= 3) & (seq4 == 1) if c == 0 else (seq >= 3) & (seq16 != 0)

    def when(condition, action):
        @pl.when(condition)
        def _():
            action()

    def send_kv(c, part):
        for ahead in (3, 1):
            across = crosses(ahead, c)
            if part == 0 and c == 1:
                when(sends(ahead, c) & jnp.logical_not(across), kv_copy(0, ahead, c, 0).start)
            elif part == 0:
                when(sends(ahead, c), kv_copy(0, ahead, c, 0).start)
            else:
                when(sends(ahead, c) & jnp.logical_not(across), kv_copy(0, ahead, c, 1).start)
                when(across, value_copy(ahead, c).start)

    def pass_values(ahead, c):
        def act():
            value_copy(ahead, c).wait_recv()
            value_pass(ahead, c).start()

        when(crossed(ahead, c), act)

    def relay(relays, back, ahead, c, some):
        def act():
            for part in (0, 1):
                kv_copy(0, back, c, part).wait_recv()
                kv_copy(back, ahead, c, part).start()

        when(relays(c) & some, act)

    def relay_on(c, some=True):
        relay(relays_on, 1, 1, c, some)

    def relay_back(c, some=True):
        relay(relays_back, 3, N_SEQ - 1, c, some)

    def kv_arrived(c):
        for part in (0, 1):
            when((seq >= 1) & jnp.logical_not(relays_on(c)), kv_copy(0, 1, c, part).wait_recv)
            when(seq >= 2, kv_copy(1, 1, c, part).wait_recv)
            when(gets(3, c) & jnp.logical_not(relays_back(c)), kv_copy(0, 3, c, part).wait_recv)

    def kv_left(c):
        for ahead in (1, 3):
            across = crosses(ahead, c)
            when(sends(ahead, c), kv_copy(0, ahead, c, 0).wait_send)
            when(sends(ahead, c) & jnp.logical_not(across), kv_copy(0, ahead, c, 1).wait_send)
            when(across, value_copy(ahead, c).wait_send)
            when(crossed(ahead, c), value_pass(ahead, c).wait_send)
        for part in (0, 1):
            when(relays_on(c), kv_copy(1, 1, c, part).wait_send)
            when(relays_back(c), kv_copy(3, N_SEQ - 1, c, part).wait_send)

    def att_copy(c):
        return remote(
            att.at[pl.ds(c * CH, CH), pl.ds(0, KV)],
            att.at[pl.ds(c * CH, CH), pl.ds(KV, KV)],
            s_at.at[c],
            r_at.at[c],
            peer(1),
        )

    def rs_copy(c):
        return remote(rs_send.at[c], rs_recv.at[c], s_rs.at[c], r_rs.at[c], peer(2))

    def st_copy(c, k):
        return remote(st_send.at[c], st_recv.at[c, k - 1], s_st.at[c, k - 1], r_st.at[c, k - 1], peer(k))

    own_copy.start()
    for k in range(2):
        for cp in w_copies(k):
            cp.start()
    pl.semaphore_wait(barrier, partners)
    for c in range(NC):
        for h in range(2):
            z_copy(c, h).start()
    sib_copy.start()
    for k in (2, 3):
        for cp in w_copies(k):
            cp.start()
    for cp in wo_copies + wo_remote:
        cp.start()

    acc[...] = jnp.zeros_like(acc)
    ss[...] = jnp.zeros_like(ss)
    o_acc[...] = jnp.zeros_like(o_acc)
    l_acc[...] = jnp.zeros_like(l_acc)
    for k in (1, 2, 3):
        @pl.when(seq < k)
        def _():
            for c in range(1 if k == 3 else 0, NC):
                kvb[c, pl.ds((3 - k) * CH, CH), :] = jnp.zeros((CH, KV), BF16)

    gi_row = gi[...].reshape(1, WIDTH)
    for i in range(8):
        gtab[i] = jnp.broadcast_to(gi_row[:, i * HALF : (i + 1) * HALF], (8, HALF))

    lane = lax.broadcasted_iota(jnp.int32, (CH, CH), 1)
    sub = lax.broadcasted_iota(jnp.int32, (CH, CH), 0)
    half_lane = jnp.where(lane >= 64, lane - 64, lane).astype(F32)
    inverse_freq = jnp.exp(half_lane * (-math.log(10000.0) / 64))
    for c in range(NC):
        p_row = pos[pl.ds(c * CH, CH)].reshape(1, CH).astype(F32)
        p_mat = jnp.broadcast_to(p_row, (CH, CH)).T
        angle = p_mat * inverse_freq
        sine = jnp.sin(angle)
        rope_c[c] = jnp.cos(angle)
        rope_s[c] = jnp.where(lane < 64, -sine, sine)
        i_rel = sub + c * CH
        low = i_rel - jnp.minimum(p_mat.astype(jnp.int32), 1023)
        for cc in range(NC):
            first = 3 if cc > c else 2
            for n in range(3):
                j_rel = CH * cc + ROWS * (n - first) + lane
                bias[c, cc, :, pl.ds(n * CH, CH)] = jnp.where((j_rel >= low) & (j_rel <= i_rel), 0.0, -1e30)

    def own_rows(wide):
        turned[...] = wide.T
        return turned.at[pl.ds(pl.multiple_of(64 * core, 64), OWN)]

    for gain, table in ((gpost, post_t), (gpre, pre_t)):
        row = gain[pl.ds(col_start(0), PAD)].reshape(1, PAD)
        table[...] = own_rows(jnp.broadcast_to(row, (CH, PAD)))[...]

    own_copy.wait()

    def step(k, c, h):
        cols = pl.ds(pl.multiple_of(c * CH, CH), CH)
        feats = pl.ds(pl.multiple_of(h * HALF, 16), HALF)
        x = xg[k, feats, cols].astype(F32)
        ss[c] += jnp.broadcast_to(jnp.sum(x * x, axis=0, keepdims=True), (8, CH))
        gain = gtab[tp_of(k) * 2 + h, pl.ds(0, 1), :]
        x = (x.T * gain).astype(BF16)
        acc[cols, pl.ds(0, 768)] += jnp.dot(x, wqv[k, feats, :], preferred_element_type=F32)
        acc[cols, pl.ds(768, 384)] += jnp.dot(x, wkv[k, feats, :], preferred_element_type=F32)
        acc[cols, pl.ds(1152, 384)] += jnp.dot(x, wvv[k, feats, :], preferred_element_type=F32)

    def local_steps(k):
        for cp in w_copies(k):
            cp.wait()

        @pl.loop(0, NC * 2)
        def _(i):
            step(k, i // 2, lax.rem(i, 2))

    local_steps(0)
    sib_copy.wait_recv()
    local_steps(1)
    for k in (2, 3):
        for cp in w_copies(k):
            cp.wait()

    def head(u, gain, c):
        mean = jnp.mean(u * u, axis=-1, keepdims=True)
        u = u * lax.rsqrt(mean + EPS) * gain
        return (u * rope_c[c] + pltpu.roll(u, 64, 1) * rope_s[c]).astype(BF16)

    def finish(c):
        rows = pl.ds(c * CH, CH)
        mean = ss[c, pl.ds(0, 1), :] / WIDTH
        scale = jnp.broadcast_to(lax.rsqrt(mean + EPS), (CH, CH)).T
        for h in range(3):
            u = acc[rows, pl.ds(768 + h * 128, 128)] * scale
            kvb[c, pl.ds(3 * CH, CH), pl.ds(h * 128, 128)] = head(u, gk[...].reshape(1, 128), c)
        send_kv(c, 0)
        for h in range(3):
            v = acc[rows, pl.ds(1152 + h * 128, 128)] * scale
            kvb[c, pl.ds(3 * CH, CH), pl.ds(384 + h * 128, 128)] = v.astype(BF16)
        send_kv(c, 1)

    def finish_q(c):
        rows = pl.ds(c * CH, CH)
        mean = ss[c, pl.ds(0, 1), :] / WIDTH
        scale = jnp.broadcast_to(lax.rsqrt(mean + EPS), (CH, CH)).T
        for h in range(3):
            for g in range(2):
                u = acc[rows, pl.ds((2 * h + g) * 128, 128)] * scale
                qs[c, h, pl.ds(g * CH, CH), :] = head(u, gq[...].reshape(1, 128), c)

    def z_step(c, h):
        z_copy(c, h).wait_recv()
        f_copy(c, h).start()
        step(2, c, h)
        f_copy(c, h).wait_recv()
        step(3, c, h)

    soon = (seq4 != 0) & jnp.logical_not(after_half)
    z_step(0, 0)
    z_step(0, 1)
    finish(0)
    finish_q(0)
    z_step(1, 0)
    relay_on(0, seq != 16)
    relay_back(0, seq != 17)
    z_step(1, 1)
    finish(1)
    finish_q(1)
    z_step(2, 0)
    relay_back(1, soon)
    z_step(2, 1)
    finish(2)
    for ahead in (3, 1):
        when(crosses(ahead, 1), kv_copy(0, ahead, 1, 0).start)
    for c in (0, 1):
        for ahead in (3, 1):
            pass_values(ahead, c)
    relay_on(0, seq == 16)
    relay_back(0, seq == 17)
    finish_q(2)

    def unit(c, cc):
        start = 0 if cc > c else CH
        b = bias[c, cc]
        b = jnp.concatenate([b, b], axis=0)
        for h in range(3):
            keys = kvb[cc, pl.ds(start, 3 * CH), pl.ds(h * 128, 128)]
            vals = kvb[cc, pl.ds(start, 3 * CH), pl.ds(384 + h * 128, 128)]
            s = lax.dot_general(qs[c, h], keys, (((1,), (1,)), ((), ())), preferred_element_type=F32)
            w = jnp.exp2(s * SCORE + b)
            l_acc[c, h] += w[:, 0:128] + w[:, 128:256] + w[:, 256:384]
            o_acc[c, h] += jnp.dot(w.astype(BF16), vals, preferred_element_type=F32)

    relay_on(1)
    relay_back(1, jnp.logical_not(soon))
    kv_arrived(0)
    for c in range(NC):
        unit(c, 0)
    for ahead in (3, 1):
        pass_values(ahead, 2)
    relay_on(2)
    relay_back(2)
    kv_arrived(1)
    for c in range(NC):
        unit(c, 1)
    kv_arrived(2)
    for cp in wo_copies:
        cp.wait()
    for cp in wo_remote:
        cp.wait()

    def project(c, i):
        return jnp.dot(att[pl.ds(c * CH, CH), :], wov[i], preferred_element_type=F32)

    for c in range(NC):
        unit(c, 2)
        for h in range(3):
            total = jnp.sum(l_acc[c, h], axis=-1, keepdims=True)
            o = (o_acc[c, h] / total).astype(BF16)
            att[pl.ds(c * CH, CH), pl.ds(2 * h * 128, 128)] = o[:CH]
            att[pl.ds(c * CH, CH), pl.ds((2 * h + 1) * 128, 128)] = o[CH:]
        att_copy(c).start()
        if c > 0:
            att_copy(c - 1).wait_recv()
            rs_send[c - 1] = own_rows(project(c - 1, 0))[...].astype(BF16)
            rs_copy(c - 1).start()
    att_copy(2).wait_recv()
    rs_send[2] = own_rows(project(2, 0))[...].astype(BF16)
    rs_copy(2).start()

    for c in range(NC):
        own[c] = own_rows(project(c, 1))[...]

    BLOCK = 64

    def stats(c):
        cols = pl.ds(c * CH, CH)
        rs_copy(c).wait_recv()

        def one(i, sums):
            rows = pl.ds(pl.multiple_of(i * BLOCK, BLOCK), BLOCK)
            s = own[c, rows, :] + rs_recv[c, rows, :].astype(F32)
            t = xg[0, rows, cols].astype(F32)
            sg = s * post_t[rows, :]
            own[c, rows, :] = s
            return tuple(
                a + jnp.sum((u * v).reshape(BLOCK // 8, 8, CH), axis=0)
                for a, u, v in zip(sums, (s, t, t, sg), (s, t, sg, sg))
            )

        sums = lax.fori_loop(0, OWN // BLOCK, one, (jnp.zeros((8, CH), F32),) * 4)
        for i, v in enumerate(sums):
            st_send[c, pl.ds(i, 1), :] = jnp.sum(v, axis=0, keepdims=True)
        for i in range(4, 8):
            st_send[c, pl.ds(i, 1), :] = jnp.zeros((1, CH), F32)
        for k in (1, 2, 3):
            st_copy(c, k).start()

    def final(c):
        cols = pl.ds(c * CH, CH)
        for k in (1, 2, 3):
            st_copy(c, k).wait_recv()
        rows4 = st_send[c] + st_recv[c, 0] + st_recv[c, 1] + st_recv[c, 2]
        post = lax.rsqrt(rows4[0:1] / WIDTH + EPS)
        square = rows4[1:2] + 2.0 * post * rows4[2:3] + post * post * rows4[3:4]
        pre = lax.rsqrt(jnp.maximum(square, 0.0) / WIDTH + EPS)

        @pl.loop(0, OWN // BLOCK)
        def _(i):
            rows = pl.ds(pl.multiple_of(i * BLOCK, BLOCK), BLOCK)
            t = xg[0, rows, cols].astype(F32)
            hidden = (t + own[c, rows, :] * post * post_t[rows, :]).astype(BF16)
            hid_v[rows, cols] = hidden
            ffn_v[rows, cols] = (hidden.astype(F32) * pre * pre_t[rows, :]).astype(BF16)

        for cp in out_copies(c):
            cp.start()

    def out_copies(c):
        cols = pl.ds(c * CH, CH)
        return [
            pltpu.make_async_copy(hid_v.at[:, cols], hid.at[:, cols], s_out.at[0, c]),
            pltpu.make_async_copy(ffn_v.at[:, cols], ffn.at[:, cols], s_out.at[1, c]),
        ]

    for c in range(NC):
        stats(c)
        if c > 0:
            final(c - 1)
    final(NC - 1)

    sib_copy.wait_send()
    for c in range(NC):
        for h in range(2):
            z_copy(c, h).wait_send()
            f_copy(c, h).wait_send()
        for k in (1, 2, 3):
            st_copy(c, k).wait_send()

        kv_left(c)
        att_copy(c).wait_send()
        rs_copy(c).wait_send()
        for cp in out_copies(c):
            cp.wait()


def copy_out(hidden, ffn_input, hid, ffn, buf, sem_in, sem_out):
    part = OWN // PARTS
    pieces = [
        (
            pltpu.make_async_copy(a.at[pl.ds(i * part, part)], buf.at[n, pl.ds(i * part, part)], sem_in.at[n, i]),
            pltpu.make_async_copy(buf.at[n, pl.ds(i * part, part)], b.at[pl.ds(i * part, part)], sem_out.at[n, i]),
        )
        for n, (a, b) in enumerate(((hidden, hid), (ffn_input, ffn)))
        for i in range(PARTS)
    ]
    for into, _ in pieces:
        into.start()
    for into, away in pieces:
        into.wait()
        away.start()
    for _, away in pieces:
        away.wait()


def local(tokens, positions, w_query, w_key, w_value, w_out, gain_input, gain_query, gain_key, gain_post, gain_pre):
    hbm = pl.BlockSpec(memory_space=pltpu.MemorySpace.HBM)
    vmem = pl.BlockSpec(memory_space=pltpu.VMEM)
    dma = pltpu.SemaphoreType.DMA
    out = jax.ShapeDtypeStruct((OWN, ROWS), BF16)
    hidden, ffn_input = pl.pallas_call(
        kernel,
        out_shape=(out, out),
        in_specs=[hbm, vmem, hbm, hbm, hbm, hbm, vmem, vmem, vmem, vmem, vmem],
        out_specs=(hbm, hbm),
        scratch_shapes=[
            pltpu.VMEM((4, OWN, ROWS), BF16),
            pltpu.VMEM((4, OWN, 768), BF16),
            pltpu.VMEM((4, OWN, 384), BF16),
            pltpu.VMEM((4, OWN, 384), BF16),
            pltpu.VMEM((2, 2 * KV, PAD), BF16),
            pltpu.VMEM((ROWS, 1536), F32),
            pltpu.VMEM((NC, 8, CH), F32),
            pltpu.VMEM((8, 8, HALF), F32),
            pltpu.VMEM((NC, CH, CH), F32),
            pltpu.VMEM((NC, CH, CH), F32),
            pltpu.VMEM((NC, NC, CH, 3 * CH), F32),
            pltpu.VMEM((NC, 3, 2 * CH, 128), BF16),
            pltpu.VMEM((NC, 4 * CH, KV), BF16),
            pltpu.VMEM((NC, 3, 2 * CH, 128), F32),
            pltpu.VMEM((NC, 3, 2 * CH, 128), F32),
            pltpu.VMEM((ROWS, 2 * KV), BF16),
            pltpu.VMEM((NC, OWN, CH), BF16),
            pltpu.VMEM((NC, OWN, CH), BF16),
            pltpu.VMEM((NC, OWN, CH), F32),
            pltpu.VMEM((OWN, CH), F32),
            pltpu.VMEM((OWN, CH), F32),
            pltpu.VMEM((PAD, CH), F32),
            pltpu.VMEM((OWN, ROWS), BF16),
            pltpu.VMEM((OWN, ROWS), BF16),
            pltpu.VMEM((NC, 8, CH), F32),
            pltpu.VMEM((NC, 3, 8, CH), F32),
            pltpu.VMEM((2, NC, CH, 384), BF16),
            dma, dma, dma,
            dma((NC, 2)), dma((NC, 2)), dma((NC, 2)), dma((NC, 2)),
            dma((3, 4)), dma((2,)), dma((2,)), dma((2,)),
            dma((4, NC, 2)), dma((3, NC, 2)),
            dma((2, NC)), dma((2, NC)), dma((2, NC)),
            dma((NC,)), dma((NC,)), dma((NC,)), dma((NC,)),
            dma((NC, 3)), dma((NC, 3)), dma((2, NC)),
        ],
        compiler_params=pltpu.CompilerParams(
            collective_id=0, has_side_effects=True, vmem_limit_bytes=60 * 1024 * 1024
        ),
        cost_estimate=pl.CostEstimate(flops=12_000_000_000, bytes_accessed=28_000_000, transcendentals=3_000_000),
    )(
        tokens.T,
        positions,
        w_query,
        w_key,
        w_value,
        w_out,
        gain_input,
        gain_query,
        gain_key,
        gain_post,
        gain_pre,
    )
    copied = pl.pallas_call(
        copy_out,
        out_shape=(out, out),
        in_specs=[hbm, hbm],
        out_specs=(hbm, hbm),
        scratch_shapes=[pltpu.VMEM((2, OWN, ROWS), BF16), dma((2, PARTS)), dma((2, PARTS))],
        compiler_params=pltpu.CompilerParams(has_side_effects=True),
    )(hidden, ffn_input)
    return copied[0].T, copied[1].T


def solution(mesh):
    torus = Mesh(mesh.devices.reshape(N_SEQ, 2, 2), ("seq", "tp_0", "tp_1"))
    tp = ("tp_0", "tp_1")
    return jax.shard_map(
        local,
        mesh=torus,
        in_specs=(
            P("seq", tp), P("seq"), P(None, tp), P(None, tp), P(None, tp), P(tp, None),
            P(), P(), P(), P(), P(),
        ),
        out_specs=(P("seq", tp), P("seq", tp)),
        check_vma=False,
    )
```

```python
import functools
import math

import jax
import jax.numpy as jnp
from jax import lax
from jax.experimental import pallas as pl
from jax.experimental.pallas import tpu as pltpu
from jax.sharding import Mesh
from jax.sharding import PartitionSpec as P

F32 = jnp.float32
BF16 = jnp.bfloat16
MESH = pl.DeviceIdType.MESH

EPS = 1e-6
WIDTH = 5376
PARTS = 4
OWN = 1344
HALF = 672
PAD = 1408
ROWS = 384
CH = 128
NC = 3
KV = 768
N_SEQ = 32
SCORE = 168.0**-0.5 * math.log2(math.e)


def kernel(
    xt, pos, wq, wk, wv, wo, gi, gq, gk, gpost, gpre,
    hid, ffn,
    xg, wqv, wkv, wvv, wov, acc, ss, gtab, rope_c, rope_s, bias,
    qs, kvb, o_acc, l_acc, att, rs_send, rs_recv, own, post_t, pre_t, turned, hid_v, ffn_v, st_send, st_recv, stage,
    s_own, s_sib, r_sib, s_z, r_z, s_f, r_f, s_w, s_wo, s_wos, r_wos,
    s_kv, r_kv, s_stage, r_stage, s_pass, s_at, r_at, s_rs, r_rs, s_st, r_st, s_out,
):
    seq = lax.axis_index("seq")
    zl = lax.axis_index("tp_0")
    core = lax.axis_index("tp_1")

    def peer(k):
        return (seq, lax.rem(zl + k // 2, 2), lax.rem(core + k % 2, 2))

    def tp_of(k):
        return lax.rem(zl + k // 2, 2) * 2 + lax.rem(core + k % 2, 2)

    def col_start(k):
        t = tp_of(k)
        return pl.multiple_of(OWN * t - 64 * lax.rem(t, 2), 128)

    def later(k, dz=0):
        return (lax.rem(seq + k, N_SEQ), lax.rem(zl + dz, 2), core)

    barrier = pltpu.get_barrier_semaphore()
    halves = jnp.where((seq >= 13) & (seq < 19), 1, 0) + jnp.where((seq == 15) | (seq == 16), 1, 0)
    partners = 3 + halves
    for k in (1, 2, 3):
        pl.semaphore_signal(barrier, inc=1, device_id=peer(k), device_id_type=MESH)
    for k in (1, 3):
        for there, step_to in ((seq + k < N_SEQ, k), (seq >= k, N_SEQ - k)):
            partners += jnp.where(there, 1, 0)

            @pl.when(there)
            def _():
                pl.semaphore_signal(barrier, inc=1, device_id=later(step_to), device_id_type=MESH)

    for there, step_to in (
        ((seq >= 13) & (seq < 16), 3),
        ((seq >= 16) & (seq < 19), N_SEQ - 3),
        (seq == 15, 1),
        (seq == 16, N_SEQ - 1),
    ):
        @pl.when(there)
        def _():
            pl.semaphore_signal(barrier, inc=1, device_id=later(step_to, 1), device_id_type=MESH)

    def remote(src, dst, ss_, rs_, dev):
        return pltpu.make_async_remote_copy(
            src_ref=src, dst_ref=dst, send_sem=ss_, recv_sem=rs_, device_id=dev, device_id_type=MESH
        )

    def piece(ref, c, h):
        return ref.at[pl.ds(h * HALF, HALF), pl.ds(c * CH, CH)]

    def z_copy(c, h):
        return remote(piece(xt, c, h), piece(xg.at[2], c, h), s_z.at[c, h], r_z.at[c, h], peer(2))

    def f_copy(c, h):
        return remote(piece(xg.at[2], c, h), piece(xg.at[3], c, h), s_f.at[c, h], r_f.at[c, h], peer(1))

    sib_copy = remote(xt, xg.at[1], s_sib, r_sib, peer(1))
    own_copy = pltpu.make_async_copy(xt, xg.at[0], s_own)

    def w_copies(k):
        first = pl.multiple_of(tp_of(k) * OWN, 16)
        return [
            pltpu.make_async_copy(a.at[pl.ds(first, OWN)], b.at[k], s_w.at[i, k])
            for i, (a, b) in enumerate(((wq, wqv), (wk, wkv), (wv, wvv)))
        ]

    wo_copies = [
        pltpu.make_async_copy(wo.at[:, pl.ds(col_start(k), PAD)], wov.at[i, pl.ds(0, KV)], s_wo.at[i])
        for i, k in enumerate((2, 0))
    ]
    wo_remote = [
        remote(wo.at[:, pl.ds(col_start(k), PAD)], wov.at[i, pl.ds(KV, KV)], s_wos.at[i], r_wos.at[i], peer(1))
        for i, k in enumerate((3, 1))
    ]

    def kv_copy(back, ahead, c, part):
        far = (back + ahead) % N_SEQ
        cols = pl.ds(384 * part, 384)
        return remote(
            kvb.at[c, pl.ds((3 - back) * CH, CH), cols],
            kvb.at[c, pl.ds((3 - far) * CH, CH), cols],
            s_kv.at[3 if back == 3 else far - 1, c, part],
            r_kv.at[far - 1, c, part],
            later(ahead),
        )

    seq4 = lax.rem(seq, 4)
    before_half = (seq >= 13) & (seq < 16)
    after_half = (seq >= 16) & (seq < 19)

    def value_copy(ahead, c):
        return remote(
            kvb.at[c, pl.ds(3 * CH, CH), pl.ds(384, 384)],
            stage.at[ahead // 2, c],
            s_stage.at[ahead // 2, c],
            r_stage.at[ahead // 2, c],
            later(ahead, 1),
        )

    def value_pass(ahead, c):
        return remote(
            stage.at[ahead // 2, c],
            kvb.at[c, pl.ds((3 - ahead) * CH, CH), pl.ds(384, 384)],
            s_pass.at[ahead // 2, c],
            r_kv.at[ahead - 1, c, 1],
            peer(2),
        )

    def sends(ahead, c):
        return (seq < N_SEQ - ahead) & (seq4 == 2) if ahead == 3 and c == 0 else seq < N_SEQ - ahead

    def gets(ahead, c):
        return (seq >= 3) & (seq4 == 1) if ahead == 3 and c == 0 else seq >= ahead

    def crosses(ahead, c):
        return seq == 15 if ahead == 1 else before_half & sends(3, c)

    def crossed(ahead, c):
        return seq == 16 if ahead == 1 else after_half & gets(3, c)

    def relays_on(c, part):
        on = (seq >= 1) & (seq < N_SEQ - 1)
        return on & (seq4 != 3) if c == 0 or part == 0 else on & (seq4 == 2)

    def relays_back(c, part):
        return (seq >= 3) & (seq4 == 1) if c == 0 or part == 0 else (seq >= 3) & (seq4 != 0)

    def when(condition, action):
        @pl.when(condition)
        def _():
            action()

    def send_kv(c, part):
        for ahead in (3, 1):
            across = crosses(ahead, c)
            if part == 0:
                when(sends(ahead, c), kv_copy(0, ahead, c, 0).start)
            else:
                straight = jnp.logical_not(across) if c < 2 else True
                when(sends(ahead, c) & straight, kv_copy(0, ahead, c, 1).start)
                if c < 2:
                    when(across, value_copy(ahead, c).start)

    def pass_values(ahead, c):
        def act():
            value_copy(ahead, c).wait_recv()
            value_pass(ahead, c).start()

        when(crossed(ahead, c), act)

    def relay(relays, back, ahead, c, part, some):
        def act():
            kv_copy(0, back, c, part).wait_recv()
            kv_copy(back, ahead, c, part).start()

        when(relays(c, part) & some, act)

    def relay_both(c, some_on=True, some_back=True):
        for part in (0, 1):
            relay(relays_on, 1, 1, c, part, some_on)
            relay(relays_back, 3, N_SEQ - 1, c, part, some_back)

    def kv_arrived(c):
        for part in (0, 1):
            when((seq >= 1) & jnp.logical_not(relays_on(c, part)), kv_copy(0, 1, c, part).wait_recv)
            when(seq >= 2, kv_copy(1, 1, c, part).wait_recv)
            when(gets(3, c) & jnp.logical_not(relays_back(c, part)), kv_copy(0, 3, c, part).wait_recv)

    def kv_left(c):
        for ahead in (1, 3):
            across = crosses(ahead, c)
            when(sends(ahead, c), kv_copy(0, ahead, c, 0).wait_send)
            straight = jnp.logical_not(across) if c < 2 else True
            when(sends(ahead, c) & straight, kv_copy(0, ahead, c, 1).wait_send)
            if c < 2:
                when(across, value_copy(ahead, c).wait_send)
                when(crossed(ahead, c), value_pass(ahead, c).wait_send)
        for part in (0, 1):
            when(relays_on(c, part), kv_copy(1, 1, c, part).wait_send)
            when(relays_back(c, part), kv_copy(3, N_SEQ - 1, c, part).wait_send)

    def att_copy(c):
        return remote(
            att.at[pl.ds(c * CH, CH), pl.ds(0, KV)],
            att.at[pl.ds(c * CH, CH), pl.ds(KV, KV)],
            s_at.at[c],
            r_at.at[c],
            peer(1),
        )

    def rs_copy(c):
        return remote(rs_send.at[c], rs_recv.at[c], s_rs.at[c], r_rs.at[c], peer(2))

    def st_copy(c, k):
        return remote(st_send.at[c], st_recv.at[c, k - 1], s_st.at[c, k - 1], r_st.at[c, k - 1], peer(k))

    own_copy.start()
    for k in range(2):
        for cp in w_copies(k):
            cp.start()
    pl.semaphore_wait(barrier, partners)
    for c in range(NC):
        for h in range(2):
            z_copy(c, h).start()
    sib_copy.start()
    for k in (2, 3):
        for cp in w_copies(k):
            cp.start()
    for cp in wo_copies + wo_remote:
        cp.start()

    acc[...] = jnp.zeros_like(acc)
    ss[...] = jnp.zeros_like(ss)
    o_acc[...] = jnp.zeros_like(o_acc)
    l_acc[...] = jnp.zeros_like(l_acc)
    for k in (1, 2, 3):
        @pl.when(seq < k)
        def _():
            for c in range(1 if k == 3 else 0, NC):
                kvb[c, pl.ds((3 - k) * CH, CH), :] = jnp.zeros((CH, KV), BF16)

    gi_row = gi[...].reshape(1, WIDTH)
    for i in range(8):
        gtab[i] = jnp.broadcast_to(gi_row[:, i * HALF : (i + 1) * HALF], (8, HALF))

    lane = lax.broadcasted_iota(jnp.int32, (CH, CH), 1)
    sub = lax.broadcasted_iota(jnp.int32, (CH, CH), 0)
    half_lane = jnp.where(lane >= 64, lane - 64, lane).astype(F32)
    inverse_freq = jnp.exp(half_lane * (-math.log(10000.0) / 64))
    for c in range(NC):
        p_row = pos[pl.ds(c * CH, CH)].reshape(1, CH).astype(F32)
        p_mat = jnp.broadcast_to(p_row, (CH, CH)).T
        angle = p_mat * inverse_freq
        sine = jnp.sin(angle)
        rope_c[c] = jnp.cos(angle)
        rope_s[c] = jnp.where(lane < 64, -sine, sine)
        i_rel = sub + c * CH
        low = i_rel - jnp.minimum(p_mat.astype(jnp.int32), 1023)
        for cc in range(NC):
            first = 3 if cc > c else 2
            for n in range(3):
                j_rel = CH * cc + ROWS * (n - first) + lane
                bias[c, cc, :, pl.ds(n * CH, CH)] = jnp.where((j_rel >= low) & (j_rel <= i_rel), 0.0, -1e30)

    def own_rows(wide):
        turned[...] = wide.T
        return turned.at[pl.ds(pl.multiple_of(64 * core, 64), OWN)]

    for gain, table in ((gpost, post_t), (gpre, pre_t)):
        row = gain[pl.ds(col_start(0), PAD)].reshape(1, PAD)
        table[...] = own_rows(jnp.broadcast_to(row, (CH, PAD)))[...]

    own_copy.wait()

    def step(k, c, h):
        cols = pl.ds(pl.multiple_of(c * CH, CH), CH)
        feats = pl.ds(pl.multiple_of(h * HALF, 16), HALF)
        x = xg[k, feats, cols].astype(F32)
        ss[c] += jnp.broadcast_to(jnp.sum(x * x, axis=0, keepdims=True), (8, CH))
        gain = gtab[tp_of(k) * 2 + h, pl.ds(0, 1), :]
        x = (x.T * gain).astype(BF16)
        acc[cols, pl.ds(0, 768)] += jnp.dot(x, wqv[k, feats, :], preferred_element_type=F32)
        acc[cols, pl.ds(768, 384)] += jnp.dot(x, wkv[k, feats, :], preferred_element_type=F32)
        acc[cols, pl.ds(1152, 384)] += jnp.dot(x, wvv[k, feats, :], preferred_element_type=F32)

    def local_steps(k):
        for cp in w_copies(k):
            cp.wait()

        @pl.loop(0, NC * 2)
        def _(i):
            step(k, i // 2, lax.rem(i, 2))

    local_steps(0)
    sib_copy.wait_recv()
    local_steps(1)
    for k in (2, 3):
        for cp in w_copies(k):
            cp.wait()

    def head(u, gain, c):
        mean = jnp.mean(u * u, axis=-1, keepdims=True)
        u = u * lax.rsqrt(mean + EPS) * gain
        return (u * rope_c[c] + pltpu.roll(u, 64, 1) * rope_s[c]).astype(BF16)

    def finish(c):
        rows = pl.ds(c * CH, CH)
        mean = ss[c, pl.ds(0, 1), :] / WIDTH
        scale = jnp.broadcast_to(lax.rsqrt(mean + EPS), (CH, CH)).T
        for h in range(3):
            u = acc[rows, pl.ds(768 + h * 128, 128)] * scale
            kvb[c, pl.ds(3 * CH, CH), pl.ds(h * 128, 128)] = head(u, gk[...].reshape(1, 128), c)
        send_kv(c, 0)
        for h in range(3):
            v = acc[rows, pl.ds(1152 + h * 128, 128)] * scale
            kvb[c, pl.ds(3 * CH, CH), pl.ds(384 + h * 128, 128)] = v.astype(BF16)
        send_kv(c, 1)

    def finish_q(c):
        rows = pl.ds(c * CH, CH)
        mean = ss[c, pl.ds(0, 1), :] / WIDTH
        scale = jnp.broadcast_to(lax.rsqrt(mean + EPS), (CH, CH)).T
        for h in range(3):
            for g in range(2):
                u = acc[rows, pl.ds((2 * h + g) * 128, 128)] * scale
                qs[c, h, pl.ds(g * CH, CH), :] = head(u, gq[...].reshape(1, 128), c)

    def z_step(c, h):
        z_copy(c, h).wait_recv()
        f_copy(c, h).start()
        step(2, c, h)
        f_copy(c, h).wait_recv()
        step(3, c, h)

    soon = (seq4 != 0) & jnp.logical_not(after_half)
    z_step(0, 0)
    z_step(0, 1)
    finish(0)
    finish_q(0)
    z_step(1, 0)
    relay_both(0, seq != 16, seq != 17)
    z_step(1, 1)
    finish(1)
    finish_q(1)
    z_step(2, 0)
    relay_both(1, soon, soon)
    z_step(2, 1)
    finish(2)
    for c in (0, 1):
        for ahead in (3, 1):
            pass_values(ahead, c)
    relay_both(0, seq == 16, seq == 17)
    finish_q(2)

    def unit(c, cc):
        start = 0 if cc > c else CH
        b = bias[c, cc]
        b = jnp.concatenate([b, b], axis=0)
        for h in range(3):
            keys = kvb[cc, pl.ds(start, 3 * CH), pl.ds(h * 128, 128)]
            vals = kvb[cc, pl.ds(start, 3 * CH), pl.ds(384 + h * 128, 128)]
            s = lax.dot_general(qs[c, h], keys, (((1,), (1,)), ((), ())), preferred_element_type=F32)
            w = jnp.exp2(s * SCORE + b)
            l_acc[c, h] += w[:, 0:128] + w[:, 128:256] + w[:, 256:384]
            o_acc[c, h] += jnp.dot(w.astype(BF16), vals, preferred_element_type=F32)

    relay_both(1, jnp.logical_not(soon), jnp.logical_not(soon))
    kv_arrived(0)
    for c in range(NC):
        unit(c, 0)
    relay_both(2)
    kv_arrived(1)
    for c in range(NC):
        unit(c, 1)
    kv_arrived(2)
    for cp in wo_copies:
        cp.wait()
    for cp in wo_remote:
        cp.wait()

    def project(c, i):
        return jnp.dot(att[pl.ds(c * CH, CH), :], wov[i], preferred_element_type=F32)

    for c in range(NC):
        unit(c, 2)
        for h in range(3):
            total = jnp.sum(l_acc[c, h], axis=-1, keepdims=True)
            o = (o_acc[c, h] / total).astype(BF16)
            att[pl.ds(c * CH, CH), pl.ds(2 * h * 128, 128)] = o[:CH]
            att[pl.ds(c * CH, CH), pl.ds((2 * h + 1) * 128, 128)] = o[CH:]
        att_copy(c).start()
        if c > 0:
            att_copy(c - 1).wait_recv()
            rs_send[c - 1] = own_rows(project(c - 1, 0))[...].astype(BF16)
            rs_copy(c - 1).start()
    att_copy(2).wait_recv()
    rs_send[2] = own_rows(project(2, 0))[...].astype(BF16)
    rs_copy(2).start()

    for c in range(NC):
        own[c] = own_rows(project(c, 1))[...]

    BLOCK = 64

    def stats(c):
        cols = pl.ds(c * CH, CH)
        rs_copy(c).wait_recv()

        def one(i, sums):
            rows = pl.ds(pl.multiple_of(i * BLOCK, BLOCK), BLOCK)
            s = own[c, rows, :] + rs_recv[c, rows, :].astype(F32)
            t = xg[0, rows, cols].astype(F32)
            sg = s * post_t[rows, :]
            own[c, rows, :] = s
            return tuple(
                a + jnp.sum((u * v).reshape(BLOCK // 8, 8, CH), axis=0)
                for a, u, v in zip(sums, (s, t, t, sg), (s, t, sg, sg))
            )

        sums = lax.fori_loop(0, OWN // BLOCK, one, (jnp.zeros((8, CH), F32),) * 4, unroll=3)
        for i, v in enumerate(sums):
            st_send[c, pl.ds(i, 1), :] = jnp.sum(v, axis=0, keepdims=True)
        for i in range(4, 8):
            st_send[c, pl.ds(i, 1), :] = jnp.zeros((1, CH), F32)
        for k in (1, 2, 3):
            st_copy(c, k).start()

    def final(c):
        cols = pl.ds(c * CH, CH)
        for k in (1, 2, 3):
            st_copy(c, k).wait_recv()
        rows4 = st_send[c] + st_recv[c, 0] + st_recv[c, 1] + st_recv[c, 2]
        post = lax.rsqrt(rows4[0:1] / WIDTH + EPS)
        square = rows4[1:2] + 2.0 * post * rows4[2:3] + post * post * rows4[3:4]
        pre = lax.rsqrt(jnp.maximum(square, 0.0) / WIDTH + EPS)

        @pl.loop(0, OWN // BLOCK, unroll=3)
        def _(i):
            rows = pl.ds(pl.multiple_of(i * BLOCK, BLOCK), BLOCK)
            t = xg[0, rows, cols].astype(F32)
            hidden = (t + own[c, rows, :] * post * post_t[rows, :]).astype(BF16)
            hid_v[rows, cols] = hidden
            ffn_v[rows, cols] = (hidden.astype(F32) * pre * pre_t[rows, :]).astype(BF16)

        for cp in out_copies(c):
            cp.start()

    def out_copies(c):
        cols = pl.ds(c * CH, CH)
        return [
            pltpu.make_async_copy(hid_v.at[:, cols], hid.at[:, cols], s_out.at[0, c]),
            pltpu.make_async_copy(ffn_v.at[:, cols], ffn.at[:, cols], s_out.at[1, c]),
        ]

    for c in range(NC):
        stats(c)
        if c > 0:
            final(c - 1)
    final(NC - 1)

    sib_copy.wait_send()
    for c in range(NC):
        for h in range(2):
            z_copy(c, h).wait_send()
            f_copy(c, h).wait_send()
        for k in (1, 2, 3):
            st_copy(c, k).wait_send()

        kv_left(c)
        att_copy(c).wait_send()
        rs_copy(c).wait_send()
        for cp in out_copies(c):
            cp.wait()


def copy_out(hidden, ffn_input, hid, ffn, buf, sem_in, sem_out):
    part = OWN // PARTS
    pieces = [
        (
            pltpu.make_async_copy(a.at[pl.ds(i * part, part)], buf.at[n, pl.ds(i * part, part)], sem_in.at[n, i]),
            pltpu.make_async_copy(buf.at[n, pl.ds(i * part, part)], b.at[pl.ds(i * part, part)], sem_out.at[n, i]),
        )
        for n, (a, b) in enumerate(((hidden, hid), (ffn_input, ffn)))
        for i in range(PARTS)
    ]
    for into, _ in pieces:
        into.start()
    for into, away in pieces:
        into.wait()
        away.start()
    for _, away in pieces:
        away.wait()


def local(tokens, positions, w_query, w_key, w_value, w_out, gain_input, gain_query, gain_key, gain_post, gain_pre):
    hbm = pl.BlockSpec(memory_space=pltpu.MemorySpace.HBM)
    vmem = pl.BlockSpec(memory_space=pltpu.VMEM)
    dma = pltpu.SemaphoreType.DMA
    out = jax.ShapeDtypeStruct((OWN, ROWS), BF16)
    hidden, ffn_input = pl.pallas_call(
        kernel,
        out_shape=(out, out),
        in_specs=[hbm, vmem, hbm, hbm, hbm, hbm, vmem, vmem, vmem, vmem, vmem],
        out_specs=(hbm, hbm),
        scratch_shapes=[
            pltpu.VMEM((4, OWN, ROWS), BF16),
            pltpu.VMEM((4, OWN, 768), BF16),
            pltpu.VMEM((4, OWN, 384), BF16),
            pltpu.VMEM((4, OWN, 384), BF16),
            pltpu.VMEM((2, 2 * KV, PAD), BF16),
            pltpu.VMEM((ROWS, 1536), F32),
            pltpu.VMEM((NC, 8, CH), F32),
            pltpu.VMEM((8, 8, HALF), F32),
            pltpu.VMEM((NC, CH, CH), F32),
            pltpu.VMEM((NC, CH, CH), F32),
            pltpu.VMEM((NC, NC, CH, 3 * CH), F32),
            pltpu.VMEM((NC, 3, 2 * CH, 128), BF16),
            pltpu.VMEM((NC, 4 * CH, KV), BF16),
            pltpu.VMEM((NC, 3, 2 * CH, 128), F32),
            pltpu.VMEM((NC, 3, 2 * CH, 128), F32),
            pltpu.VMEM((ROWS, 2 * KV), BF16),
            pltpu.VMEM((NC, OWN, CH), BF16),
            pltpu.VMEM((NC, OWN, CH), BF16),
            pltpu.VMEM((NC, OWN, CH), F32),
            pltpu.VMEM((OWN, CH), F32),
            pltpu.VMEM((OWN, CH), F32),
            pltpu.VMEM((PAD, CH), F32),
            pltpu.VMEM((OWN, ROWS), BF16),
            pltpu.VMEM((OWN, ROWS), BF16),
            pltpu.VMEM((NC, 8, CH), F32),
            pltpu.VMEM((NC, 3, 8, CH), F32),
            pltpu.VMEM((2, NC, CH, 384), BF16),
            dma, dma, dma,
            dma((NC, 2)), dma((NC, 2)), dma((NC, 2)), dma((NC, 2)),
            dma((3, 4)), dma((2,)), dma((2,)), dma((2,)),
            dma((4, NC, 2)), dma((3, NC, 2)),
            dma((2, NC)), dma((2, NC)), dma((2, NC)),
            dma((NC,)), dma((NC,)), dma((NC,)), dma((NC,)),
            dma((NC, 3)), dma((NC, 3)), dma((2, NC)),
        ],
        compiler_params=pltpu.CompilerParams(
            collective_id=0, has_side_effects=True, vmem_limit_bytes=60 * 1024 * 1024
        ),
        cost_estimate=pl.CostEstimate(flops=12_000_000_000, bytes_accessed=28_000_000, transcendentals=3_000_000),
    )(
        tokens.T,
        positions,
        w_query,
        w_key,
        w_value,
        w_out,
        gain_input,
        gain_query,
        gain_key,
        gain_post,
        gain_pre,
    )
    copied = pl.pallas_call(
        copy_out,
        out_shape=(out, out),
        in_specs=[hbm, hbm],
        out_specs=(hbm, hbm),
        scratch_shapes=[pltpu.VMEM((2, OWN, ROWS), BF16), dma((2, PARTS)), dma((2, PARTS))],
        compiler_params=pltpu.CompilerParams(has_side_effects=True),
    )(hidden, ffn_input)
    return copied[0].T, copied[1].T


def solution(mesh):
    torus = Mesh(mesh.devices.reshape(N_SEQ, 2, 2), ("seq", "tp_0", "tp_1"))
    tp = ("tp_0", "tp_1")
    return jax.shard_map(
        local,
        mesh=torus,
        in_specs=(
            P("seq", tp), P("seq"), P(None, tp), P(None, tp), P(None, tp), P(tp, None),
            P(), P(), P(), P(), P(),
        ),
        out_specs=(P("seq", tp), P("seq", tp)),
        check_vma=False,
    )
```

```python
import functools
import math

import jax
import jax.numpy as jnp
from jax import lax
from jax.experimental import pallas as pl
from jax.experimental.pallas import tpu as pltpu
from jax.sharding import Mesh
from jax.sharding import PartitionSpec as P

F32 = jnp.float32
BF16 = jnp.bfloat16
MESH = pl.DeviceIdType.MESH

EPS = 1e-6
WIDTH = 5376
PARTS = 4
OWN = 1344
HALF = 672
PAD = 1408
ROWS = 384
CH = 128
NC = 3
KV = 768
N_SEQ = 32
SCORE = 168.0**-0.5 * math.log2(math.e)


def kernel(
    xt, pos, wq, wk, wv, wo, gi, gq, gk, gpost, gpre,
    hid, ffn,
    xg, wqv, wkv, wvv, wov, acc, ss, gtab, rope_c, rope_s, bias,
    qs, kvb, o_acc, l_acc, att, rs_send, rs_recv, own, post_t, pre_t, turned, hid_v, ffn_v, st_send, st_recv, stage,
    s_own, s_sib, r_sib, s_z, r_z, s_f, r_f, s_w, s_wo, s_wos, r_wos,
    s_kv, r_kv, s_stage, r_stage, s_pass, s_at, r_at, s_rs, r_rs, s_st, r_st, s_out,
):
    seq = lax.axis_index("seq")
    zl = lax.axis_index("tp_0")
    core = lax.axis_index("tp_1")

    def peer(k):
        return (seq, lax.rem(zl + k // 2, 2), lax.rem(core + k % 2, 2))

    def tp_of(k):
        return lax.rem(zl + k // 2, 2) * 2 + lax.rem(core + k % 2, 2)

    def col_start(k):
        t = tp_of(k)
        return pl.multiple_of(OWN * t - 64 * lax.rem(t, 2), 128)

    def later(k, dz=0):
        return (lax.rem(seq + k, N_SEQ), lax.rem(zl + dz, 2), core)

    barrier = pltpu.get_barrier_semaphore()
    halves = jnp.where((seq >= 13) & (seq < 19), 1, 0) + jnp.where((seq == 15) | (seq == 16), 1, 0)
    partners = 3 + halves
    for k in (1, 2, 3):
        pl.semaphore_signal(barrier, inc=1, device_id=peer(k), device_id_type=MESH)
    for k in (1, 3):
        for there, step_to in ((seq + k < N_SEQ, k), (seq >= k, N_SEQ - k)):
            partners += jnp.where(there, 1, 0)

            @pl.when(there)
            def _():
                pl.semaphore_signal(barrier, inc=1, device_id=later(step_to), device_id_type=MESH)

    for there, step_to in (
        ((seq >= 13) & (seq < 16), 3),
        ((seq >= 16) & (seq < 19), N_SEQ - 3),
        (seq == 15, 1),
        (seq == 16, N_SEQ - 1),
    ):
        @pl.when(there)
        def _():
            pl.semaphore_signal(barrier, inc=1, device_id=later(step_to, 1), device_id_type=MESH)

    def remote(src, dst, ss_, rs_, dev):
        return pltpu.make_async_remote_copy(
            src_ref=src, dst_ref=dst, send_sem=ss_, recv_sem=rs_, device_id=dev, device_id_type=MESH
        )

    def piece(ref, c, h):
        return ref.at[pl.ds(h * HALF, HALF), pl.ds(c * CH, CH)]

    def z_copy(c, h):
        return remote(piece(xt, c, h), piece(xg.at[2], c, h), s_z.at[c, h], r_z.at[c, h], peer(2))

    def f_copy(c, h):
        return remote(piece(xg.at[2], c, h), piece(xg.at[3], c, h), s_f.at[c, h], r_f.at[c, h], peer(1))

    sib_copy = remote(xt, xg.at[1], s_sib, r_sib, peer(1))
    own_copy = pltpu.make_async_copy(xt, xg.at[0], s_own)

    def w_copies(k):
        first = pl.multiple_of(tp_of(k) * OWN, 16)
        return [
            pltpu.make_async_copy(a.at[pl.ds(first, OWN)], b.at[k], s_w.at[i, k])
            for i, (a, b) in enumerate(((wq, wqv), (wk, wkv), (wv, wvv)))
        ]

    wo_copies = [
        pltpu.make_async_copy(wo.at[:, pl.ds(col_start(k), PAD)], wov.at[i, pl.ds(0, KV)], s_wo.at[i])
        for i, k in enumerate((2, 0))
    ]
    wo_remote = [
        remote(wo.at[:, pl.ds(col_start(k), PAD)], wov.at[i, pl.ds(KV, KV)], s_wos.at[i], r_wos.at[i], peer(1))
        for i, k in enumerate((3, 1))
    ]

    def kv_copy(back, ahead, c, part):
        far = (back + ahead) % N_SEQ
        cols = pl.ds(384 * part, 384)
        return remote(
            kvb.at[c, pl.ds((3 - back) * CH, CH), cols],
            kvb.at[c, pl.ds((3 - far) * CH, CH), cols],
            s_kv.at[3 if back == 3 else far - 1, c, part],
            r_kv.at[far - 1, c, part],
            later(ahead),
        )

    seq4 = lax.rem(seq, 4)
    before_half = (seq >= 13) & (seq < 16)
    after_half = (seq >= 16) & (seq < 19)

    def value_copy(ahead, c):
        return remote(
            kvb.at[c, pl.ds(3 * CH, CH), pl.ds(384, 384)],
            stage.at[ahead // 2, c],
            s_stage.at[ahead // 2, c],
            r_stage.at[ahead // 2, c],
            later(ahead, 1),
        )

    def value_pass(ahead, c):
        return remote(
            stage.at[ahead // 2, c],
            kvb.at[c, pl.ds((3 - ahead) * CH, CH), pl.ds(384, 384)],
            s_pass.at[ahead // 2, c],
            r_kv.at[ahead - 1, c, 1],
            peer(2),
        )

    def sends(ahead, c):
        return (seq < N_SEQ - ahead) & (seq4 == 2) if ahead == 3 and c == 0 else seq < N_SEQ - ahead

    def gets(ahead, c):
        return (seq >= 3) & (seq4 == 1) if ahead == 3 and c == 0 else seq >= ahead

    def crosses(ahead, c):
        return seq == 15 if ahead == 1 else before_half & sends(3, c)

    def crossed(ahead, c):
        return seq == 16 if ahead == 1 else after_half & gets(3, c)

    def relays_on(c, part):
        on = (seq >= 1) & (seq < N_SEQ - 1)
        if c == 2 and part == 1:
            return on & (seq4 >= 2)
        return on & (seq4 != 3) if c == 0 or part == 0 else on & (seq4 == 2)

    def relays_back(c, part):
        if c == 2 and part == 1:
            return (seq >= 3) & (seq4 >= 2)
        return (seq >= 3) & (seq4 == 1) if c == 0 or part == 0 else (seq >= 3) & (seq4 != 0)

    def when(condition, action):
        @pl.when(condition)
        def _():
            action()

    def send_kv(c, part):
        for ahead in (3, 1):
            across = crosses(ahead, c)
            if part == 0:
                when(sends(ahead, c), kv_copy(0, ahead, c, 0).start)
            else:
                straight = jnp.logical_not(across) if c < 2 else True
                when(sends(ahead, c) & straight, kv_copy(0, ahead, c, 1).start)
                if c < 2:
                    when(across, value_copy(ahead, c).start)

    def pass_values(ahead, c):
        def act():
            value_copy(ahead, c).wait_recv()
            value_pass(ahead, c).start()

        when(crossed(ahead, c), act)

    def relay(relays, back, ahead, c, part, some):
        def act():
            kv_copy(0, back, c, part).wait_recv()
            kv_copy(back, ahead, c, part).start()

        when(relays(c, part) & some, act)

    def relay_both(c, some_on=True, some_back=True):
        for part in (0, 1):
            relay(relays_on, 1, 1, c, part, some_on)
            relay(relays_back, 3, N_SEQ - 1, c, part, some_back)

    def kv_arrived(c):
        for part in (0, 1):
            when((seq >= 1) & jnp.logical_not(relays_on(c, part)), kv_copy(0, 1, c, part).wait_recv)
            when(seq >= 2, kv_copy(1, 1, c, part).wait_recv)
            when(gets(3, c) & jnp.logical_not(relays_back(c, part)), kv_copy(0, 3, c, part).wait_recv)

    def kv_left(c):
        for ahead in (1, 3):
            across = crosses(ahead, c)
            when(sends(ahead, c), kv_copy(0, ahead, c, 0).wait_send)
            straight = jnp.logical_not(across) if c < 2 else True
            when(sends(ahead, c) & straight, kv_copy(0, ahead, c, 1).wait_send)
            if c < 2:
                when(across, value_copy(ahead, c).wait_send)
                when(crossed(ahead, c), value_pass(ahead, c).wait_send)
        for part in (0, 1):
            when(relays_on(c, part), kv_copy(1, 1, c, part).wait_send)
            when(relays_back(c, part), kv_copy(3, N_SEQ - 1, c, part).wait_send)

    def att_copy(c):
        return remote(
            att.at[pl.ds(c * CH, CH), pl.ds(0, KV)],
            att.at[pl.ds(c * CH, CH), pl.ds(KV, KV)],
            s_at.at[c],
            r_at.at[c],
            peer(1),
        )

    def rs_copy(c):
        return remote(rs_send.at[c], rs_recv.at[c], s_rs.at[c], r_rs.at[c], peer(2))

    def st_copy(c, k):
        return remote(st_send.at[c], st_recv.at[c, k - 1], s_st.at[c, k - 1], r_st.at[c, k - 1], peer(k))

    own_copy.start()
    for k in range(2):
        for cp in w_copies(k):
            cp.start()
    pl.semaphore_wait(barrier, partners)
    for c in range(NC):
        for h in range(2):
            z_copy(c, h).start()
    sib_copy.start()
    for k in (2, 3):
        for cp in w_copies(k):
            cp.start()
    for cp in wo_copies + wo_remote:
        cp.start()

    acc[...] = jnp.zeros_like(acc)
    ss[...] = jnp.zeros_like(ss)
    o_acc[...] = jnp.zeros_like(o_acc)
    l_acc[...] = jnp.zeros_like(l_acc)
    for k in (1, 2, 3):
        @pl.when(seq < k)
        def _():
            for c in range(1 if k == 3 else 0, NC):
                kvb[c, pl.ds((3 - k) * CH, CH), :] = jnp.zeros((CH, KV), BF16)

    gi_row = gi[...].reshape(1, WIDTH)
    for i in range(8):
        gtab[i] = jnp.broadcast_to(gi_row[:, i * HALF : (i + 1) * HALF], (8, HALF))

    lane = lax.broadcasted_iota(jnp.int32, (CH, CH), 1)
    sub = lax.broadcasted_iota(jnp.int32, (CH, CH), 0)
    half_lane = jnp.where(lane >= 64, lane - 64, lane).astype(F32)
    inverse_freq = jnp.exp(half_lane * (-math.log(10000.0) / 64))
    for c in range(NC):
        p_row = pos[pl.ds(c * CH, CH)].reshape(1, CH).astype(F32)
        p_mat = jnp.broadcast_to(p_row, (CH, CH)).T
        angle = p_mat * inverse_freq
        sine = jnp.sin(angle)
        rope_c[c] = jnp.cos(angle)
        rope_s[c] = jnp.where(lane < 64, -sine, sine)
        i_rel = sub + c * CH
        low = i_rel - jnp.minimum(p_mat.astype(jnp.int32), 1023)
        for cc in range(NC):
            first = 3 if cc > c else 2
            for n in range(3):
                j_rel = CH * cc + ROWS * (n - first) + lane
                bias[c, cc, :, pl.ds(n * CH, CH)] = jnp.where((j_rel >= low) & (j_rel <= i_rel), 0.0, -1e30)

    def own_rows(wide):
        turned[...] = wide.T
        return turned.at[pl.ds(pl.multiple_of(64 * core, 64), OWN)]

    for gain, table in ((gpost, post_t), (gpre, pre_t)):
        row = gain[pl.ds(col_start(0), PAD)].reshape(1, PAD)
        table[...] = own_rows(jnp.broadcast_to(row, (CH, PAD)))[...]

    own_copy.wait()

    def step(k, c, h):
        cols = pl.ds(pl.multiple_of(c * CH, CH), CH)
        feats = pl.ds(pl.multiple_of(h * HALF, 16), HALF)
        x = xg[k, feats, cols].astype(F32)
        ss[c] += jnp.broadcast_to(jnp.sum(x * x, axis=0, keepdims=True), (8, CH))
        gain = gtab[tp_of(k) * 2 + h, pl.ds(0, 1), :]
        x = (x.T * gain).astype(BF16)
        acc[cols, pl.ds(0, 768)] += jnp.dot(x, wqv[k, feats, :], preferred_element_type=F32)
        acc[cols, pl.ds(768, 384)] += jnp.dot(x, wkv[k, feats, :], preferred_element_type=F32)
        acc[cols, pl.ds(1152, 384)] += jnp.dot(x, wvv[k, feats, :], preferred_element_type=F32)

    def local_steps(k):
        for cp in w_copies(k):
            cp.wait()

        @pl.loop(0, NC * 2)
        def _(i):
            step(k, i // 2, lax.rem(i, 2))

    local_steps(0)
    sib_copy.wait_recv()
    local_steps(1)
    for k in (2, 3):
        for cp in w_copies(k):
            cp.wait()

    def head(u, gain, c):
        mean = jnp.mean(u * u, axis=-1, keepdims=True)
        u = u * lax.rsqrt(mean + EPS) * gain
        return (u * rope_c[c] + pltpu.roll(u, 64, 1) * rope_s[c]).astype(BF16)

    def finish(c):
        rows = pl.ds(c * CH, CH)
        mean = ss[c, pl.ds(0, 1), :] / WIDTH
        scale = jnp.broadcast_to(lax.rsqrt(mean + EPS), (CH, CH)).T
        for h in range(3):
            u = acc[rows, pl.ds(768 + h * 128, 128)] * scale
            kvb[c, pl.ds(3 * CH, CH), pl.ds(h * 128, 128)] = head(u, gk[...].reshape(1, 128), c)
        send_kv(c, 0)
        for h in range(3):
            v = acc[rows, pl.ds(1152 + h * 128, 128)] * scale
            kvb[c, pl.ds(3 * CH, CH), pl.ds(384 + h * 128, 128)] = v.astype(BF16)
        send_kv(c, 1)

    def finish_q(c):
        rows = pl.ds(c * CH, CH)
        mean = ss[c, pl.ds(0, 1), :] / WIDTH
        scale = jnp.broadcast_to(lax.rsqrt(mean + EPS), (CH, CH)).T
        for h in range(3):
            for g in range(2):
                u = acc[rows, pl.ds((2 * h + g) * 128, 128)] * scale
                qs[c, h, pl.ds(g * CH, CH), :] = head(u, gq[...].reshape(1, 128), c)

    def z_step(c, h):
        z_copy(c, h).wait_recv()
        f_copy(c, h).start()
        step(2, c, h)
        f_copy(c, h).wait_recv()
        step(3, c, h)

    soon = (seq4 != 0) & jnp.logical_not(after_half)
    z_step(0, 0)
    z_step(0, 1)
    finish(0)
    finish_q(0)
    z_step(1, 0)
    relay_both(0, seq != 16, seq != 17)
    z_step(1, 1)
    finish(1)
    finish_q(1)
    z_step(2, 0)
    relay_both(1, soon, soon)
    z_step(2, 1)
    finish(2)
    for c in (0, 1):
        for ahead in (3, 1):
            pass_values(ahead, c)
    relay_both(0, seq == 16, seq == 17)
    finish_q(2)

    def unit(c, cc):
        start = 0 if cc > c else CH
        b = bias[c, cc]
        b = jnp.concatenate([b, b], axis=0)
        for h in range(3):
            keys = kvb[cc, pl.ds(start, 3 * CH), pl.ds(h * 128, 128)]
            vals = kvb[cc, pl.ds(start, 3 * CH), pl.ds(384 + h * 128, 128)]
            s = lax.dot_general(qs[c, h], keys, (((1,), (1,)), ((), ())), preferred_element_type=F32)
            w = jnp.exp2(s * SCORE + b)
            l_acc[c, h] += w[:, 0:128] + w[:, 128:256] + w[:, 256:384]
            o_acc[c, h] += jnp.dot(w.astype(BF16), vals, preferred_element_type=F32)

    relay_both(1, jnp.logical_not(soon), jnp.logical_not(soon))
    kv_arrived(0)
    for c in range(NC):
        unit(c, 0)
    relay_both(2)
    kv_arrived(1)
    for c in range(NC):
        unit(c, 1)
    kv_arrived(2)
    for cp in wo_copies:
        cp.wait()
    for cp in wo_remote:
        cp.wait()

    def project(c, i):
        return jnp.dot(att[pl.ds(c * CH, CH), :], wov[i], preferred_element_type=F32)

    def project_half(c, i, part):
        cols = pl.ds(part * KV, KV)
        return jnp.dot(att[pl.ds(c * CH, CH), cols], wov[i, cols, :], preferred_element_type=F32)

    for c in range(NC):
        unit(c, 2)
        for h in range(3):
            total = jnp.sum(l_acc[c, h], axis=-1, keepdims=True)
            o = (o_acc[c, h] / total).astype(BF16)
            att[pl.ds(c * CH, CH), pl.ds(2 * h * 128, 128)] = o[:CH]
            att[pl.ds(c * CH, CH), pl.ds((2 * h + 1) * 128, 128)] = o[CH:]
        att_copy(c).start()
        first = project_half(c, 0, 0)
        att_copy(c).wait_recv()
        rs_send[c] = own_rows(first + project_half(c, 0, 1))[...].astype(BF16)
        rs_copy(c).start()

    for c in range(NC):
        own[c] = own_rows(project(c, 1))[...]

    BLOCK = 64

    def stats(c):
        cols = pl.ds(c * CH, CH)
        rs_copy(c).wait_recv()

        def one(i, sums):
            rows = pl.ds(pl.multiple_of(i * BLOCK, BLOCK), BLOCK)
            s = own[c, rows, :] + rs_recv[c, rows, :].astype(F32)
            t = xg[0, rows, cols].astype(F32)
            sg = s * post_t[rows, :]
            own[c, rows, :] = s
            return tuple(
                a + jnp.sum((u * v).reshape(BLOCK // 8, 8, CH), axis=0)
                for a, u, v in zip(sums, (s, t, t, sg), (s, t, sg, sg))
            )

        sums = lax.fori_loop(0, OWN // BLOCK, one, (jnp.zeros((8, CH), F32),) * 4, unroll=3)
        for i, v in enumerate(sums):
            st_send[c, pl.ds(i, 1), :] = jnp.sum(v, axis=0, keepdims=True)
        for i in range(4, 8):
            st_send[c, pl.ds(i, 1), :] = jnp.zeros((1, CH), F32)
        for k in (1, 2, 3):
            st_copy(c, k).start()

    def final(c):
        cols = pl.ds(c * CH, CH)
        for k in (1, 2, 3):
            st_copy(c, k).wait_recv()
        rows4 = st_send[c] + st_recv[c, 0] + st_recv[c, 1] + st_recv[c, 2]
        post = lax.rsqrt(rows4[0:1] / WIDTH + EPS)
        square = rows4[1:2] + 2.0 * post * rows4[2:3] + post * post * rows4[3:4]
        pre = lax.rsqrt(jnp.maximum(square, 0.0) / WIDTH + EPS)

        @pl.loop(0, OWN // BLOCK, unroll=3)
        def _(i):
            rows = pl.ds(pl.multiple_of(i * BLOCK, BLOCK), BLOCK)
            t = xg[0, rows, cols].astype(F32)
            hidden = (t + own[c, rows, :] * post * post_t[rows, :]).astype(BF16)
            hid_v[rows, cols] = hidden
            ffn_v[rows, cols] = (hidden.astype(F32) * pre * pre_t[rows, :]).astype(BF16)

        for cp in out_copies(c):
            cp.start()

    def out_copies(c):
        cols = pl.ds(c * CH, CH)
        return [
            pltpu.make_async_copy(hid_v.at[:, cols], hid.at[:, cols], s_out.at[0, c]),
            pltpu.make_async_copy(ffn_v.at[:, cols], ffn.at[:, cols], s_out.at[1, c]),
        ]

    for c in range(NC):
        stats(c)
        if c > 0:
            final(c - 1)
    final(NC - 1)

    sib_copy.wait_send()
    for c in range(NC):
        for h in range(2):
            z_copy(c, h).wait_send()
            f_copy(c, h).wait_send()
        for k in (1, 2, 3):
            st_copy(c, k).wait_send()

        kv_left(c)
        att_copy(c).wait_send()
        rs_copy(c).wait_send()
        for cp in out_copies(c):
            cp.wait()


def copy_out(hidden, ffn_input, hid, ffn, buf, sem_in, sem_out):
    part = OWN // PARTS
    pieces = [
        (
            pltpu.make_async_copy(a.at[pl.ds(i * part, part)], buf.at[n, pl.ds(i * part, part)], sem_in.at[n, i]),
            pltpu.make_async_copy(buf.at[n, pl.ds(i * part, part)], b.at[pl.ds(i * part, part)], sem_out.at[n, i]),
        )
        for n, (a, b) in enumerate(((hidden, hid), (ffn_input, ffn)))
        for i in range(PARTS)
    ]
    for into, _ in pieces:
        into.start()
    for into, away in pieces:
        into.wait()
        away.start()
    for _, away in pieces:
        away.wait()


def local(tokens, positions, w_query, w_key, w_value, w_out, gain_input, gain_query, gain_key, gain_post, gain_pre):
    hbm = pl.BlockSpec(memory_space=pltpu.MemorySpace.HBM)
    vmem = pl.BlockSpec(memory_space=pltpu.VMEM)
    dma = pltpu.SemaphoreType.DMA
    out = jax.ShapeDtypeStruct((OWN, ROWS), BF16)
    hidden, ffn_input = pl.pallas_call(
        kernel,
        out_shape=(out, out),
        in_specs=[hbm, vmem, hbm, hbm, hbm, hbm, vmem, vmem, vmem, vmem, vmem],
        out_specs=(hbm, hbm),
        scratch_shapes=[
            pltpu.VMEM((4, OWN, ROWS), BF16),
            pltpu.VMEM((4, OWN, 768), BF16),
            pltpu.VMEM((4, OWN, 384), BF16),
            pltpu.VMEM((4, OWN, 384), BF16),
            pltpu.VMEM((2, 2 * KV, PAD), BF16),
            pltpu.VMEM((ROWS, 1536), F32),
            pltpu.VMEM((NC, 8, CH), F32),
            pltpu.VMEM((8, 8, HALF), F32),
            pltpu.VMEM((NC, CH, CH), F32),
            pltpu.VMEM((NC, CH, CH), F32),
            pltpu.VMEM((NC, NC, CH, 3 * CH), F32),
            pltpu.VMEM((NC, 3, 2 * CH, 128), BF16),
            pltpu.VMEM((NC, 4 * CH, KV), BF16),
            pltpu.VMEM((NC, 3, 2 * CH, 128), F32),
            pltpu.VMEM((NC, 3, 2 * CH, 128), F32),
            pltpu.VMEM((ROWS, 2 * KV), BF16),
            pltpu.VMEM((NC, OWN, CH), BF16),
            pltpu.VMEM((NC, OWN, CH), BF16),
            pltpu.VMEM((NC, OWN, CH), F32),
            pltpu.VMEM((OWN, CH), F32),
            pltpu.VMEM((OWN, CH), F32),
            pltpu.VMEM((PAD, CH), F32),
            pltpu.VMEM((OWN, ROWS), BF16),
            pltpu.VMEM((OWN, ROWS), BF16),
            pltpu.VMEM((NC, 8, CH), F32),
            pltpu.VMEM((NC, 3, 8, CH), F32),
            pltpu.VMEM((2, NC, CH, 384), BF16),
            dma, dma, dma,
            dma((NC, 2)), dma((NC, 2)), dma((NC, 2)), dma((NC, 2)),
            dma((3, 4)), dma((2,)), dma((2,)), dma((2,)),
            dma((4, NC, 2)), dma((3, NC, 2)),
            dma((2, NC)), dma((2, NC)), dma((2, NC)),
            dma((NC,)), dma((NC,)), dma((NC,)), dma((NC,)),
            dma((NC, 3)), dma((NC, 3)), dma((2, NC)),
        ],
        compiler_params=pltpu.CompilerParams(
            collective_id=0, has_side_effects=True, vmem_limit_bytes=60 * 1024 * 1024
        ),
        cost_estimate=pl.CostEstimate(flops=12_000_000_000, bytes_accessed=28_000_000, transcendentals=3_000_000),
    )(
        tokens.T,
        positions,
        w_query,
        w_key,
        w_value,
        w_out,
        gain_input,
        gain_query,
        gain_key,
        gain_post,
        gain_pre,
    )
    copied = pl.pallas_call(
        copy_out,
        out_shape=(out, out),
        in_specs=[hbm, hbm],
        out_specs=(hbm, hbm),
        scratch_shapes=[pltpu.VMEM((2, OWN, ROWS), BF16), dma((2, PARTS)), dma((2, PARTS))],
        compiler_params=pltpu.CompilerParams(has_side_effects=True),
    )(hidden, ffn_input)
    return copied[0].T, copied[1].T


def solution(mesh):
    torus = Mesh(mesh.devices.reshape(N_SEQ, 2, 2), ("seq", "tp_0", "tp_1"))
    tp = ("tp_0", "tp_1")
    return jax.shard_map(
        local,
        mesh=torus,
        in_specs=(
            P("seq", tp), P("seq"), P(None, tp), P(None, tp), P(None, tp), P(tp, None),
            P(), P(), P(), P(), P(),
        ),
        out_specs=(P("seq", tp), P("seq", tp)),
        check_vma=False,
    )
```

```python
import functools
import math

import jax
import jax.numpy as jnp
from jax import lax
from jax.experimental import pallas as pl
from jax.experimental.pallas import tpu as pltpu
from jax.sharding import Mesh
from jax.sharding import PartitionSpec as P

F32 = jnp.float32
BF16 = jnp.bfloat16
MESH = pl.DeviceIdType.MESH

EPS = 1e-6
WIDTH = 5376
PARTS = 4
OWN = 1344
HALF = 672
PAD = 1408
ROWS = 384
CH = 128
NC = 3
KV = 768
N_SEQ = 32
PIECES = (((0, 672), (672, 672)), ((0, 672), (672, 672)), ((0, 672), (672, 336), (1008, 336)))
SCORE = 168.0**-0.5 * math.log2(math.e)


def kernel(
    xt, pos, wq, wk, wv, wo, gi, gq, gk, gpost, gpre,
    hid, ffn,
    xg, wqv, wkv, wvv, wov, acc, ss, gtab, rope_c, rope_s, bias,
    qs, kvb, o_acc, l_acc, att, rs_send, rs_recv, own, post_t, pre_t, turned, hid_v, ffn_v, st_send, st_recv, stage,
    s_own, s_sib, r_sib, s_z, r_z, s_f, r_f, s_w, s_wo, s_wos, r_wos,
    s_kv, r_kv, s_stage, r_stage, s_pass, s_at, r_at, s_rs, r_rs, s_st, r_st, s_out,
):
    seq = lax.axis_index("seq")
    zl = lax.axis_index("tp_0")
    core = lax.axis_index("tp_1")

    def peer(k):
        return (seq, lax.rem(zl + k // 2, 2), lax.rem(core + k % 2, 2))

    def tp_of(k):
        return lax.rem(zl + k // 2, 2) * 2 + lax.rem(core + k % 2, 2)

    def col_start(k):
        t = tp_of(k)
        return pl.multiple_of(OWN * t - 64 * lax.rem(t, 2), 128)

    def later(k, dz=0):
        return (lax.rem(seq + k, N_SEQ), lax.rem(zl + dz, 2), core)

    barrier = pltpu.get_barrier_semaphore()
    halves = jnp.where((seq >= 13) & (seq < 19), 1, 0) + jnp.where((seq == 15) | (seq == 16), 1, 0)
    partners = 3 + halves
    for k in (1, 2, 3):
        pl.semaphore_signal(barrier, inc=1, device_id=peer(k), device_id_type=MESH)
    for k in (1, 3):
        for there, step_to in ((seq + k < N_SEQ, k), (seq >= k, N_SEQ - k)):
            partners += jnp.where(there, 1, 0)

            @pl.when(there)
            def _():
                pl.semaphore_signal(barrier, inc=1, device_id=later(step_to), device_id_type=MESH)

    for there, step_to in (
        ((seq >= 13) & (seq < 16), 3),
        ((seq >= 16) & (seq < 19), N_SEQ - 3),
        (seq == 15, 1),
        (seq == 16, N_SEQ - 1),
    ):
        @pl.when(there)
        def _():
            pl.semaphore_signal(barrier, inc=1, device_id=later(step_to, 1), device_id_type=MESH)

    def remote(src, dst, ss_, rs_, dev):
        return pltpu.make_async_remote_copy(
            src_ref=src, dst_ref=dst, send_sem=ss_, recv_sem=rs_, device_id=dev, device_id_type=MESH
        )

    def piece(ref, c, h):
        return ref.at[pl.ds(*PIECES[c][h]), pl.ds(c * CH, CH)]

    def z_copy(c, h):
        return remote(piece(xt, c, h), piece(xg.at[2], c, h), s_z.at[c, h], r_z.at[c, h], peer(2))

    def f_copy(c, h):
        return remote(piece(xg.at[2], c, h), piece(xg.at[3], c, h), s_f.at[c, h], r_f.at[c, h], peer(1))

    sib_copy = remote(xt, xg.at[1], s_sib, r_sib, peer(1))
    own_copy = pltpu.make_async_copy(xt, xg.at[0], s_own)

    def w_copies(k):
        first = pl.multiple_of(tp_of(k) * OWN, 16)
        return [
            pltpu.make_async_copy(a.at[pl.ds(first, OWN)], b.at[k], s_w.at[i, k])
            for i, (a, b) in enumerate(((wq, wqv), (wk, wkv), (wv, wvv)))
        ]

    wo_copies = [
        pltpu.make_async_copy(wo.at[:, pl.ds(col_start(k), PAD)], wov.at[i, pl.ds(0, KV)], s_wo.at[i])
        for i, k in enumerate((2, 0))
    ]
    wo_remote = [
        remote(wo.at[:, pl.ds(col_start(k), PAD)], wov.at[i, pl.ds(KV, KV)], s_wos.at[i], r_wos.at[i], peer(1))
        for i, k in enumerate((3, 1))
    ]

    def kv_copy(back, ahead, c, part):
        far = (back + ahead) % N_SEQ
        cols = pl.ds(384 * part, 384)
        return remote(
            kvb.at[c, pl.ds((3 - back) * CH, CH), cols],
            kvb.at[c, pl.ds((3 - far) * CH, CH), cols],
            s_kv.at[3 if back == 3 else far - 1, c, part],
            r_kv.at[far - 1, c, part],
            later(ahead),
        )

    seq4 = lax.rem(seq, 4)
    before_half = (seq >= 13) & (seq < 16)
    after_half = (seq >= 16) & (seq < 19)

    def value_copy(ahead, c):
        return remote(
            kvb.at[c, pl.ds(3 * CH, CH), pl.ds(384, 384)],
            stage.at[ahead // 2, c],
            s_stage.at[ahead // 2, c],
            r_stage.at[ahead // 2, c],
            later(ahead, 1),
        )

    def value_pass(ahead, c):
        return remote(
            stage.at[ahead // 2, c],
            kvb.at[c, pl.ds((3 - ahead) * CH, CH), pl.ds(384, 384)],
            s_pass.at[ahead // 2, c],
            r_kv.at[ahead - 1, c, 1],
            peer(2),
        )

    def sends(ahead, c):
        return (seq < N_SEQ - ahead) & (seq4 == 2) if ahead == 3 and c == 0 else seq < N_SEQ - ahead

    def gets(ahead, c):
        return (seq >= 3) & (seq4 == 1) if ahead == 3 and c == 0 else seq >= ahead

    def crosses(ahead, c):
        return seq == 15 if ahead == 1 else before_half & sends(3, c)

    def crossed(ahead, c):
        return seq == 16 if ahead == 1 else after_half & gets(3, c)

    def relays_on(c, part):
        on = (seq >= 1) & (seq < N_SEQ - 1)
        if c == 2 and part == 1:
            return on & (seq4 >= 2)
        return on & (seq4 != 3) if c == 0 or part == 0 else on & (seq4 == 2)

    def relays_back(c, part):
        if c == 2 and part == 1:
            return (seq >= 3) & (seq4 >= 2)
        return (seq >= 3) & (seq4 == 1) if c == 0 or part == 0 else (seq >= 3) & (seq4 != 0)

    def when(condition, action):
        @pl.when(condition)
        def _():
            action()

    def send_kv(c, part):
        for ahead in (3, 1):
            across = crosses(ahead, c)
            if part == 0:
                when(sends(ahead, c), kv_copy(0, ahead, c, 0).start)
            else:
                straight = jnp.logical_not(across) if c < 2 else True
                when(sends(ahead, c) & straight, kv_copy(0, ahead, c, 1).start)
                if c < 2:
                    when(across, value_copy(ahead, c).start)

    def pass_values(ahead, c):
        def act():
            value_copy(ahead, c).wait_recv()
            value_pass(ahead, c).start()

        when(crossed(ahead, c), act)

    def relay(relays, back, ahead, c, part, some):
        def act():
            kv_copy(0, back, c, part).wait_recv()
            kv_copy(back, ahead, c, part).start()

        when(relays(c, part) & some, act)

    def relay_both(c, some_on=True, some_back=True):
        for part in (0, 1):
            relay(relays_on, 1, 1, c, part, some_on)
            relay(relays_back, 3, N_SEQ - 1, c, part, some_back)

    def kv_arrived(c):
        for part in (0, 1):
            when((seq >= 1) & jnp.logical_not(relays_on(c, part)), kv_copy(0, 1, c, part).wait_recv)
            when(seq >= 2, kv_copy(1, 1, c, part).wait_recv)
            when(gets(3, c) & jnp.logical_not(relays_back(c, part)), kv_copy(0, 3, c, part).wait_recv)

    def kv_left(c):
        for ahead in (1, 3):
            across = crosses(ahead, c)
            when(sends(ahead, c), kv_copy(0, ahead, c, 0).wait_send)
            straight = jnp.logical_not(across) if c < 2 else True
            when(sends(ahead, c) & straight, kv_copy(0, ahead, c, 1).wait_send)
            if c < 2:
                when(across, value_copy(ahead, c).wait_send)
                when(crossed(ahead, c), value_pass(ahead, c).wait_send)
        for part in (0, 1):
            when(relays_on(c, part), kv_copy(1, 1, c, part).wait_send)
            when(relays_back(c, part), kv_copy(3, N_SEQ - 1, c, part).wait_send)

    def att_copy(c):
        return remote(
            att.at[pl.ds(c * CH, CH), pl.ds(0, KV)],
            att.at[pl.ds(c * CH, CH), pl.ds(KV, KV)],
            s_at.at[c],
            r_at.at[c],
            peer(1),
        )

    def rs_copy(c):
        return remote(rs_send.at[c], rs_recv.at[c], s_rs.at[c], r_rs.at[c], peer(2))

    def st_copy(c, k):
        return remote(st_send.at[c], st_recv.at[c, k - 1], s_st.at[c, k - 1], r_st.at[c, k - 1], peer(k))

    own_copy.start()
    for k in range(2):
        for cp in w_copies(k):
            cp.start()
    pl.semaphore_wait(barrier, partners)
    for c in range(NC):
        for h in range(len(PIECES[c])):
            z_copy(c, h).start()
    sib_copy.start()
    for k in (2, 3):
        for cp in w_copies(k):
            cp.start()
    for cp in wo_copies + wo_remote:
        cp.start()

    acc[...] = jnp.zeros_like(acc)
    ss[...] = jnp.zeros_like(ss)
    o_acc[...] = jnp.zeros_like(o_acc)
    l_acc[...] = jnp.zeros_like(l_acc)
    for k in (1, 2, 3):
        @pl.when(seq < k)
        def _():
            for c in range(1 if k == 3 else 0, NC):
                kvb[c, pl.ds((3 - k) * CH, CH), :] = jnp.zeros((CH, KV), BF16)

    gi_row = gi[...].reshape(1, WIDTH)
    for i in range(8):
        gtab[i] = jnp.broadcast_to(gi_row[:, i * HALF : (i + 1) * HALF], (8, HALF))

    lane = lax.broadcasted_iota(jnp.int32, (CH, CH), 1)
    sub = lax.broadcasted_iota(jnp.int32, (CH, CH), 0)
    half_lane = jnp.where(lane >= 64, lane - 64, lane).astype(F32)
    inverse_freq = jnp.exp(half_lane * (-math.log(10000.0) / 64))
    for c in range(NC):
        p_row = pos[pl.ds(c * CH, CH)].reshape(1, CH).astype(F32)
        p_mat = jnp.broadcast_to(p_row, (CH, CH)).T
        angle = p_mat * inverse_freq
        sine = jnp.sin(angle)
        rope_c[c] = jnp.cos(angle)
        rope_s[c] = jnp.where(lane < 64, -sine, sine)
        i_rel = sub + c * CH
        low = i_rel - jnp.minimum(p_mat.astype(jnp.int32), 1023)
        for cc in range(NC):
            first = 3 if cc > c else 2
            for n in range(3):
                j_rel = CH * cc + ROWS * (n - first) + lane
                bias[c, cc, :, pl.ds(n * CH, CH)] = jnp.where((j_rel >= low) & (j_rel <= i_rel), 0.0, -1e30)

    def own_rows(wide):
        turned[...] = wide.T
        return turned.at[pl.ds(pl.multiple_of(64 * core, 64), OWN)]

    for gain, table in ((gpost, post_t), (gpre, pre_t)):
        row = gain[pl.ds(col_start(0), PAD)].reshape(1, PAD)
        table[...] = own_rows(jnp.broadcast_to(row, (CH, PAD)))[...]

    own_copy.wait()

    def step(k, c, h, part=(0, HALF)):
        cols = pl.ds(pl.multiple_of(c * CH, CH), CH)
        feats = pl.ds(pl.multiple_of(h * HALF + part[0], 16), part[1])
        x = xg[k, feats, cols].astype(F32)
        ss[c] += jnp.broadcast_to(jnp.sum(x * x, axis=0, keepdims=True), (8, CH))
        gain = gtab[tp_of(k) * 2 + h, pl.ds(0, 1), :][:, part[0] : part[0] + part[1]]
        x = (x.T * gain).astype(BF16)
        acc[cols, pl.ds(0, 768)] += jnp.dot(x, wqv[k, feats, :], preferred_element_type=F32)
        acc[cols, pl.ds(768, 384)] += jnp.dot(x, wkv[k, feats, :], preferred_element_type=F32)
        acc[cols, pl.ds(1152, 384)] += jnp.dot(x, wvv[k, feats, :], preferred_element_type=F32)

    def local_steps(k):
        for cp in w_copies(k):
            cp.wait()

        @pl.loop(0, NC * 2)
        def _(i):
            step(k, i // 2, lax.rem(i, 2))

    local_steps(0)
    sib_copy.wait_recv()
    local_steps(1)
    for k in (2, 3):
        for cp in w_copies(k):
            cp.wait()

    def head(u, gain, c):
        mean = jnp.mean(u * u, axis=-1, keepdims=True)
        u = u * lax.rsqrt(mean + EPS) * gain
        return (u * rope_c[c] + pltpu.roll(u, 64, 1) * rope_s[c]).astype(BF16)

    def finish(c):
        rows = pl.ds(c * CH, CH)
        mean = ss[c, pl.ds(0, 1), :] / WIDTH
        scale = jnp.broadcast_to(lax.rsqrt(mean + EPS), (CH, CH)).T
        for h in range(3):
            u = acc[rows, pl.ds(768 + h * 128, 128)] * scale
            kvb[c, pl.ds(3 * CH, CH), pl.ds(h * 128, 128)] = head(u, gk[...].reshape(1, 128), c)
        send_kv(c, 0)
        for h in range(3):
            v = acc[rows, pl.ds(1152 + h * 128, 128)] * scale
            kvb[c, pl.ds(3 * CH, CH), pl.ds(384 + h * 128, 128)] = v.astype(BF16)
        send_kv(c, 1)

    def finish_q(c):
        rows = pl.ds(c * CH, CH)
        mean = ss[c, pl.ds(0, 1), :] / WIDTH
        scale = jnp.broadcast_to(lax.rsqrt(mean + EPS), (CH, CH)).T
        for h in range(3):
            for g in range(2):
                u = acc[rows, pl.ds((2 * h + g) * 128, 128)] * scale
                qs[c, h, pl.ds(g * CH, CH), :] = head(u, gq[...].reshape(1, 128), c)

    def z_step(c, h):
        z_copy(c, h).wait_recv()
        f_copy(c, h).start()
        first, size = PIECES[c][h]
        place = (c, first // HALF, (first % HALF, size))
        step(2, *place)
        f_copy(c, h).wait_recv()
        step(3, *place)

    soon = (seq4 != 0) & jnp.logical_not(after_half)
    z_step(0, 0)
    z_step(0, 1)
    finish(0)
    finish_q(0)
    z_step(1, 0)
    relay_both(0, seq != 16, seq != 17)
    z_step(1, 1)
    finish(1)
    finish_q(1)
    z_step(2, 0)
    relay_both(1, soon, soon)
    z_step(2, 1)
    z_step(2, 2)
    finish(2)
    for c in (0, 1):
        for ahead in (3, 1):
            pass_values(ahead, c)
    relay_both(0, seq == 16, seq == 17)
    finish_q(2)

    def unit(c, cc):
        start = 0 if cc > c else CH
        b = bias[c, cc]
        b = jnp.concatenate([b, b], axis=0)
        for h in range(3):
            keys = kvb[cc, pl.ds(start, 3 * CH), pl.ds(h * 128, 128)]
            vals = kvb[cc, pl.ds(start, 3 * CH), pl.ds(384 + h * 128, 128)]
            s = lax.dot_general(qs[c, h], keys, (((1,), (1,)), ((), ())), preferred_element_type=F32)
            w = jnp.exp2(s * SCORE + b)
            l_acc[c, h] += w[:, 0:128] + w[:, 128:256] + w[:, 256:384]
            o_acc[c, h] += jnp.dot(w.astype(BF16), vals, preferred_element_type=F32)

    relay_both(1, jnp.logical_not(soon), jnp.logical_not(soon))
    kv_arrived(0)
    for c in range(NC):
        unit(c, 0)
    relay_both(2)
    kv_arrived(1)
    for c in range(NC):
        unit(c, 1)
    kv_arrived(2)
    for cp in wo_copies:
        cp.wait()
    for cp in wo_remote:
        cp.wait()

    def project(c, i):
        return jnp.dot(att[pl.ds(c * CH, CH), :], wov[i], preferred_element_type=F32)

    def project_half(c, i, part):
        cols = pl.ds(part * KV, KV)
        return jnp.dot(att[pl.ds(c * CH, CH), cols], wov[i, cols, :], preferred_element_type=F32)

    for c in range(NC):
        unit(c, 2)
        for h in range(3):
            total = jnp.sum(l_acc[c, h], axis=-1, keepdims=True)
            o = (o_acc[c, h] / total).astype(BF16)
            att[pl.ds(c * CH, CH), pl.ds(2 * h * 128, 128)] = o[:CH]
            att[pl.ds(c * CH, CH), pl.ds((2 * h + 1) * 128, 128)] = o[CH:]
        att_copy(c).start()
        first = project_half(c, 0, 0)
        att_copy(c).wait_recv()
        rs_send[c] = own_rows(first + project_half(c, 0, 1))[...].astype(BF16)
        rs_copy(c).start()

    for c in range(NC):
        own[c] = own_rows(project(c, 1))[...]

    BLOCK = 64

    def stats(c):
        cols = pl.ds(c * CH, CH)
        rs_copy(c).wait_recv()

        def one(i, sums):
            rows = pl.ds(pl.multiple_of(i * BLOCK, BLOCK), BLOCK)
            s = own[c, rows, :] + rs_recv[c, rows, :].astype(F32)
            t = xg[0, rows, cols].astype(F32)
            sg = s * post_t[rows, :]
            own[c, rows, :] = s
            return tuple(
                a + jnp.sum((u * v).reshape(BLOCK // 8, 8, CH), axis=0)
                for a, u, v in zip(sums, (s, t, t, sg), (s, t, sg, sg))
            )

        sums = lax.fori_loop(0, OWN // BLOCK, one, (jnp.zeros((8, CH), F32),) * 4, unroll=3)
        for i, v in enumerate(sums):
            st_send[c, pl.ds(i, 1), :] = jnp.sum(v, axis=0, keepdims=True)
        for i in range(4, 8):
            st_send[c, pl.ds(i, 1), :] = jnp.zeros((1, CH), F32)
        for k in (1, 2, 3):
            st_copy(c, k).start()

    def final(c):
        cols = pl.ds(c * CH, CH)
        for k in (1, 2, 3):
            st_copy(c, k).wait_recv()
        rows4 = st_send[c] + st_recv[c, 0] + st_recv[c, 1] + st_recv[c, 2]
        post = lax.rsqrt(rows4[0:1] / WIDTH + EPS)
        square = rows4[1:2] + 2.0 * post * rows4[2:3] + post * post * rows4[3:4]
        pre = lax.rsqrt(jnp.maximum(square, 0.0) / WIDTH + EPS)

        @pl.loop(0, OWN // BLOCK, unroll=3)
        def _(i):
            rows = pl.ds(pl.multiple_of(i * BLOCK, BLOCK), BLOCK)
            t = xg[0, rows, cols].astype(F32)
            hidden = (t + own[c, rows, :] * post * post_t[rows, :]).astype(BF16)
            hid_v[rows, cols] = hidden
            ffn_v[rows, cols] = (hidden.astype(F32) * pre * pre_t[rows, :]).astype(BF16)

        for cp in out_copies(c):
            cp.start()

    def out_copies(c):
        cols = pl.ds(c * CH, CH)
        return [
            pltpu.make_async_copy(hid_v.at[:, cols], hid.at[:, cols], s_out.at[0, c]),
            pltpu.make_async_copy(ffn_v.at[:, cols], ffn.at[:, cols], s_out.at[1, c]),
        ]

    for c in range(NC):
        stats(c)
        if c > 0:
            final(c - 1)
    final(NC - 1)

    sib_copy.wait_send()
    for c in range(NC):
        for h in range(len(PIECES[c])):
            z_copy(c, h).wait_send()
            f_copy(c, h).wait_send()
        for k in (1, 2, 3):
            st_copy(c, k).wait_send()

        kv_left(c)
        att_copy(c).wait_send()
        rs_copy(c).wait_send()
        for cp in out_copies(c):
            cp.wait()


def copy_out(hidden, ffn_input, hid, ffn, buf, sem_in, sem_out):
    part = OWN // PARTS
    pieces = [
        (
            pltpu.make_async_copy(a.at[pl.ds(i * part, part)], buf.at[n, pl.ds(i * part, part)], sem_in.at[n, i]),
            pltpu.make_async_copy(buf.at[n, pl.ds(i * part, part)], b.at[pl.ds(i * part, part)], sem_out.at[n, i]),
        )
        for n, (a, b) in enumerate(((hidden, hid), (ffn_input, ffn)))
        for i in range(PARTS)
    ]
    for into, _ in pieces:
        into.start()
    for into, away in pieces:
        into.wait()
        away.start()
    for _, away in pieces:
        away.wait()


def local(tokens, positions, w_query, w_key, w_value, w_out, gain_input, gain_query, gain_key, gain_post, gain_pre):
    hbm = pl.BlockSpec(memory_space=pltpu.MemorySpace.HBM)
    vmem = pl.BlockSpec(memory_space=pltpu.VMEM)
    dma = pltpu.SemaphoreType.DMA
    out = jax.ShapeDtypeStruct((OWN, ROWS), BF16)
    hidden, ffn_input = pl.pallas_call(
        kernel,
        out_shape=(out, out),
        in_specs=[hbm, vmem, hbm, hbm, hbm, hbm, vmem, vmem, vmem, vmem, vmem],
        out_specs=(hbm, hbm),
        scratch_shapes=[
            pltpu.VMEM((4, OWN, ROWS), BF16),
            pltpu.VMEM((4, OWN, 768), BF16),
            pltpu.VMEM((4, OWN, 384), BF16),
            pltpu.VMEM((4, OWN, 384), BF16),
            pltpu.VMEM((2, 2 * KV, PAD), BF16),
            pltpu.VMEM((ROWS, 1536), F32),
            pltpu.VMEM((NC, 8, CH), F32),
            pltpu.VMEM((8, 8, HALF), F32),
            pltpu.VMEM((NC, CH, CH), F32),
            pltpu.VMEM((NC, CH, CH), F32),
            pltpu.VMEM((NC, NC, CH, 3 * CH), F32),
            pltpu.VMEM((NC, 3, 2 * CH, 128), BF16),
            pltpu.VMEM((NC, 4 * CH, KV), BF16),
            pltpu.VMEM((NC, 3, 2 * CH, 128), F32),
            pltpu.VMEM((NC, 3, 2 * CH, 128), F32),
            pltpu.VMEM((ROWS, 2 * KV), BF16),
            pltpu.VMEM((NC, OWN, CH), BF16),
            pltpu.VMEM((NC, OWN, CH), BF16),
            pltpu.VMEM((NC, OWN, CH), F32),
            pltpu.VMEM((OWN, CH), F32),
            pltpu.VMEM((OWN, CH), F32),
            pltpu.VMEM((PAD, CH), F32),
            pltpu.VMEM((OWN, ROWS), BF16),
            pltpu.VMEM((OWN, ROWS), BF16),
            pltpu.VMEM((NC, 8, CH), F32),
            pltpu.VMEM((NC, 3, 8, CH), F32),
            pltpu.VMEM((2, NC, CH, 384), BF16),
            dma, dma, dma,
            dma((NC, 3)), dma((NC, 3)), dma((NC, 3)), dma((NC, 3)),
            dma((3, 4)), dma((2,)), dma((2,)), dma((2,)),
            dma((4, NC, 2)), dma((3, NC, 2)),
            dma((2, NC)), dma((2, NC)), dma((2, NC)),
            dma((NC,)), dma((NC,)), dma((NC,)), dma((NC,)),
            dma((NC, 3)), dma((NC, 3)), dma((2, NC)),
        ],
        compiler_params=pltpu.CompilerParams(
            collective_id=0, has_side_effects=True, vmem_limit_bytes=60 * 1024 * 1024
        ),
        cost_estimate=pl.CostEstimate(flops=12_000_000_000, bytes_accessed=28_000_000, transcendentals=3_000_000),
    )(
        tokens.T,
        positions,
        w_query,
        w_key,
        w_value,
        w_out,
        gain_input,
        gain_query,
        gain_key,
        gain_post,
        gain_pre,
    )
    copied = pl.pallas_call(
        copy_out,
        out_shape=(out, out),
        in_specs=[hbm, hbm],
        out_specs=(hbm, hbm),
        scratch_shapes=[pltpu.VMEM((2, OWN, ROWS), BF16), dma((2, PARTS)), dma((2, PARTS))],
        compiler_params=pltpu.CompilerParams(has_side_effects=True),
    )(hidden, ffn_input)
    return copied[0].T, copied[1].T


def solution(mesh):
    torus = Mesh(mesh.devices.reshape(N_SEQ, 2, 2), ("seq", "tp_0", "tp_1"))
    tp = ("tp_0", "tp_1")
    return jax.shard_map(
        local,
        mesh=torus,
        in_specs=(
            P("seq", tp), P("seq"), P(None, tp), P(None, tp), P(None, tp), P(tp, None),
            P(), P(), P(), P(), P(),
        ),
        out_specs=(P("seq", tp), P("seq", tp)),
        check_vma=False,
    )
```
